32 devices in a mesh: grp: 4 (over y, core), mem: 8 (over z, x).
Axes of the slice: x: 2, y: 2, z: 4, core: 2. Of those that a mesh axis runs over, the one named last changes fastest.
Arguments:
- spectral: bfloat16 [512, 3, 2, 256, 192], P('grp', None, None, 'mem'), may hold values from -6 to 6
- inverse: bfloat16 [512, 48, 192], P('grp'), may hold values from -0.4375 to 0.4375
- legendre: bfloat16 [256, 64, 512], P('mem', None, 'grp'), may hold values from -0.015625 to 0.015625
- vorticity: bfloat16 [3, 64, 48, 1536], P(None, 'mem', 'grp'), may hold values from -6 to 6
- degree_list: int32 [512], replicated, may hold values from 0 to 511, as said below
- order_map: int32 [256], replicated, may hold values from 0 to 255, as said below
Outputs:
- advection: bfloat16 [3, 64, 48, 1536], P(None, 'mem', 'grp')
The draws below stay inside these ranges and needn't reach their ends.
Inputs may be any that keep to these rules, and one draw needn't show every extreme that they name: `degree_list`: a permutation of the degrees; slots 2j and 2j + 1 hold a degree d and 511 - d. `order_map`: a permutation of the orders; slots 2j and 2j + 1 hold an order m and 255 - m.
All inputs are finite; a program needn't handle non-finite values.
Results may differ from the reference program's by a relative error of at most 0.0062.
Values may be sent and summed in bfloat16 or wider, within the bound.
A program may use at most 64 MiB of HBM per device.

```python
import math
import jax
import jax.numpy as jnp

L = 512
M = 256
R = 192
NPHI = 1536
NSH = 48
NLAT = 64


def paired_slots(key, count):
    lower = jax.random.permutation(key, count // 2).astype(jnp.int32)
    joined = jnp.stack([lower, count - 1 - lower], axis=1)
    return joined.reshape(count).astype(jnp.int32)


def draw_degree_list(key, part):
    return paired_slots(jax.random.fold_in(key, 11), L)


def draw_order_map(key, part):
    return paired_slots(jax.random.fold_in(key, 23), M)


def levels(key, dims, shards, smallest, high):
    factor_of = 1.0
    for dim, shards_of in shards:
        heights = jax.random.uniform(jax.random.fold_in(jax.random.fold_in(key, 6), dim), (shards_of,), jnp.float32, smallest / len(shards), high / len(shards))
        factor_of = factor_of * jnp.repeat(jnp.exp(heights), dims[dim] // shards_of).reshape((-1,) + (1,) * (len(dims) - 1 - dim))
    return factor_of


def noise(stream_key, shape, scale, bound, cuts=(), held_as=jnp.bfloat16):
    values = scale * jax.random.normal(stream_key, shape, jnp.float32)
    if cuts:
        values = values * levels(stream_key, shape, cuts, -0.22, 0.18)
    return jnp.clip(values, -bound, bound).astype(held_as)


def setup_inputs(seed: int = 0) -> dict:
    key_of = jax.random.split(jax.random.key(seed), 7)
    spectral = noise(key_of[0], (L, 3, 2, M, R), 1.0, 6.0, ((0, 4), (3, 8)))
    inverse = noise(key_of[1], (L, NSH, R), R ** -0.5, 0.4375, ((0, 4),))
    legendre = noise(key_of[2], (M, NLAT, L), (L * M) ** -0.5, 0.015625, ((0, 8), (2, 4)))
    vorticity = noise(key_of[3], (3, NLAT, NSH, NPHI), 1.0, 6.0, ((1, 8), (2, 4)))
    degree_list = draw_degree_list(jax.random.fold_in(key_of[6], 71), 0)
    order_map = draw_order_map(jax.random.fold_in(key_of[6], 71), 0)
    return dict(spectral=spectral, inverse=inverse, legendre=legendre, vorticity=vorticity, degree_list=degree_list, order_map=order_map)


def cross_product(flow_velocity, vorticity):
    other = vorticity.astype(jnp.float32)
    first = flow_velocity[:, :, 1] * other[2] - flow_velocity[:, :, 2] * other[1]
    second = flow_velocity[:, :, 2] * other[0] - flow_velocity[:, :, 0] * other[2]
    third = flow_velocity[:, :, 0] * other[1] - flow_velocity[:, :, 1] * other[0]
    return jnp.stack([first, second, third]).astype(jnp.bfloat16)


def fourier_table(order_map, count):
    longitude = jnp.arange(count, dtype=jnp.int32)
    phase = (order_map[:, None] * longitude[None, :]) % count
    angle = phase.astype(jnp.float32) * (2.0 * math.pi / count)
    weight = jnp.where(order_map == 0, 1.0, 2.0).astype(jnp.float32)[:, None]
    return jnp.stack([weight * jnp.cos(angle), -weight * jnp.sin(angle)], axis=1).astype(jnp.bfloat16)


def reference(spectral, inverse, legendre, vorticity, degree_list, order_map):
    valid = (degree_list[:, None] >= order_map[None, :]).astype(jnp.int32)
    radial_factor = jnp.einsum("agt,aefzt->agefz", inverse.astype(jnp.float32), spectral.astype(jnp.float32)).astype(jnp.bfloat16)
    table = legendre.astype(jnp.float32) * jnp.transpose(valid).astype(jnp.float32)[:, None, :]
    latitudinal = jnp.einsum("mtl,lsckm->mtsck", table, radial_factor.astype(jnp.float32)).astype(jnp.bfloat16)
    trig = fourier_table(order_map, NPHI)
    flow_velocity = jnp.einsum("mtsck,mkp->tscp", latitudinal.astype(jnp.float32), trig.astype(jnp.float32))
    return cross_product(flow_velocity, vorticity)
```

```python
import functools
import math

import jax
import jax.numpy as jnp
from jax import lax
from jax.experimental import pallas as pl
from jax.experimental.pallas import tpu as pltpu
from jax.sharding import PartitionSpec as P

F32 = jnp.float32
BF16 = jnp.bfloat16
LANES = 128
NT = (((1,), (1,)), ((), ()))
NN = (((1,), (0,)), ((), ()))


def nt(a, b):
    return lax.dot_general(a, b, NT, preferred_element_type=F32)


def nn(a, b):
    return lax.dot_general(a, b, NN, preferred_element_type=F32)


def cross_product(flow_velocity, vorticity):
    other = vorticity.astype(jnp.float32)
    first = flow_velocity[:, :, 1] * other[2] - flow_velocity[:, :, 2] * other[1]
    second = flow_velocity[:, :, 2] * other[0] - flow_velocity[:, :, 0] * other[2]
    third = flow_velocity[:, :, 0] * other[1] - flow_velocity[:, :, 1] * other[0]
    return jnp.stack([first, second, third]).astype(jnp.bfloat16)


def fourier_table(order_map, count):
    longitude = jnp.arange(count, dtype=jnp.int32)
    phase = order_map[:, None] * longitude[None, :] % count
    angle = phase.astype(jnp.float32) * (2.0 * math.pi / count)
    weight = jnp.where(order_map == 0, 1.0, 2.0).astype(jnp.float32)[:, None]
    return jnp.stack([weight * jnp.cos(angle), -weight * jnp.sin(angle)], axis=1).astype(
        jnp.bfloat16
    )


def plain_shards(spectral, inverse, legendre, vorticity, degree_list, order_map):
    orders = spectral.shape[3]
    shells = vorticity.shape[2]
    local_order_list = lax.dynamic_slice_in_dim(
        order_map, lax.axis_index("mem") * orders, orders
    )
    width = spectral.shape[0]
    flat = spectral.reshape(width, 6 * orders, spectral.shape[4])
    solved = lax.dot_general(
        inverse, flat, (((2,), (2,)), ((0,), (0,))), preferred_element_type=F32
    ).astype(BF16)
    moved = lax.all_to_all(solved, "grp", split_axis=1, concat_axis=0, tiled=True)
    by_order = jnp.transpose(
        moved.reshape(moved.shape[0], moved.shape[1] * 6, orders), (2, 0, 1)
    )
    segment = lax.all_gather(legendre, "grp", axis=2, tiled=True)
    allowed = local_order_list[:, None] <= degree_list[None, :]
    table = jnp.where(allowed[:, None, :], segment, jnp.zeros_like(segment))
    latitudinal = lax.dot_general(
        table, by_order, (((2,), (1,)), ((0,), (0,))), preferred_element_type=F32
    ).astype(BF16)
    gathered = lax.all_to_all(latitudinal, "mem", split_axis=1, concat_axis=0, tiled=True)
    arranged = gathered.reshape(gathered.shape[0], gathered.shape[1], shells, 3, 2)
    trig = fourier_table(order_map, vorticity.shape[3])
    velocity = jnp.einsum("mtsck,mkp->tscp", arranged, trig, preferred_element_type=F32)
    return cross_product(velocity, vorticity)


def synth_body(
    groups, members, spec_hbm, inv_hbm, leg_ref, deg_ref, ord_ref, send_ref,
    spec, inv, t0, t1, t2, i0, i1, i2, i3, solved, f0, f1, f2, sems,
):
    orders, radii, width = spec.shape[2:]
    shells = inv.shape[0]
    lats = leg_ref.shape[1]
    half = LANES // 2
    fill = 2 * LANES - radii
    rows = 3 * orders
    mine = shells // groups
    per_tile = LANES // orders

    inv_copy = pltpu.make_async_copy(inv_hbm, inv, sems.at[3])
    inv_copy.start()
    copies = [pltpu.make_async_copy(spec_hbm.at[c], spec.at[c], sems.at[c]) for c in range(3)]
    for copy in copies:
        copy.start()

    eye = (
        lax.broadcasted_iota(jnp.int32, (width, width), 0)
        == lax.broadcasted_iota(jnp.int32, (width, width), 1)
    ).astype(BF16)
    gap = jnp.zeros((fill, width), BF16)

    inv_copy.wait()

    def turn_inverse(s, carry):
        a = inv[s]
        out = nt(eye, jnp.concatenate([a, gap, gap, a], axis=0))
        at = pl.ds(pl.multiple_of(s * width, width), width)
        i0[at, :] = out[:, 0:LANES]
        i1[at, :] = out[:, LANES : 2 * LANES]
        i2[at, :] = out[:, 2 * LANES : 3 * LANES]
        i3[at, :] = out[:, 3 * LANES : 4 * LANES]
        return carry

    lax.fori_loop(0, shells, turn_inverse, 0, unroll=4)

    for c in range(3):
        copies[c].wait()

        def turn_profiles(m, carry):
            out = nt(eye, jnp.concatenate([spec[c, 0, m], spec[c, 1, m]], axis=0))
            at = pl.ds(pl.multiple_of((c * orders + m) * width, width), width)
            t0[at, :] = out[:, 0:LANES]
            t1[at, :] = out[:, LANES : 2 * LANES]
            t2[at, :] = out[:, 2 * LANES : 3 * LANES]
            return carry

        lax.fori_loop(0, orders, turn_profiles, 0, unroll=4)

    nothing = jnp.zeros((shells, LANES), BF16)
    pad = jnp.zeros((half - shells, 3 * LANES), BF16)

    def solve(l, carry):
        at = pl.ds(l, rows, stride=width)
        profiles = jnp.concatenate([r[at, :].astype(BF16) for r in (t0, t1, t2)], axis=1)
        on = pl.ds(l, shells, stride=width)
        real = jnp.concatenate([i0[on, :].astype(BF16), i1[on, :].astype(BF16), nothing], axis=1)
        imag = jnp.concatenate([nothing, i2[on, :].astype(BF16), i3[on, :].astype(BF16)], axis=1)
        solved[at, :] = nt(profiles, jnp.concatenate([real, pad, imag, pad], axis=0))
        return carry

    lax.fori_loop(0, width, solve, 0, unroll=4)

    degrees = deg_ref[...]

    def sum_degrees(m, carry):
        table = jnp.where(degrees >= ord_ref[m], leg_ref[m].astype(F32), 0.0).astype(BF16)
        block = jnp.concatenate(
            [
                solved[pl.ds(pl.multiple_of((c * orders + m) * width, width), width), :].astype(BF16)
                for c in range(3)
            ],
            axis=1,
        )
        out = nn(table, block)
        at = pl.ds(m, lats, stride=orders)
        f0[at, :] = out[:, 0:LANES]
        f1[at, :] = out[:, LANES : 2 * LANES]
        f2[at, :] = out[:, 2 * LANES : 3 * LANES]
        return carry

    lax.fori_loop(0, orders, sum_degrees, 0, unroll=4)

    row = lax.broadcasted_iota(jnp.int32, (2 * shells, LANES), 0)
    lane = lax.broadcasted_iota(jnp.int32, (2 * shells, LANES), 1)
    want = row
    for i in range(1, 2 * groups):
        g, k = i // 2, i % 2
        step = (half + g * mine - i * mine) if k else (g * mine - i * mine)
        want = jnp.where(row >= i * mine, row + step, want)
    pick = (want == lane).astype(BF16)
    tiles = lats // members // per_tile

    def turn_sums(j, carry):
        parts = []
        for b in range(tiles):
            at = pl.ds(pl.multiple_of((j * tiles + b) * LANES, LANES), LANES)
            parts += [nt(pick, f[at, :].astype(BF16)) for f in (f0, f1, f2)]
        for g in range(groups):
            block = [p[g * 2 * mine : (g + 1) * 2 * mine] for p in parts]
            send_ref[j, g] = jnp.concatenate(block, axis=0).astype(BF16)
        return carry

    lax.fori_loop(0, members, turn_sums, 0)


def synthesize(spec, inv, legendre, degrees, orders_here, groups, members):
    _, _, orders, radii, width = spec.shape
    shells = inv.shape[0]
    lats = legendre.shape[1]
    mine = shells // groups
    block = lats // members * orders * mine * 6 // LANES
    any_space = pl.BlockSpec(memory_space=pl.ANY)
    vmem = pl.BlockSpec(memory_space=pltpu.VMEM)
    return pl.pallas_call(
        functools.partial(synth_body, groups, members),
        out_shape=jax.ShapeDtypeStruct((members, groups, block, LANES), BF16),
        in_specs=[any_space, any_space, vmem, vmem, pl.BlockSpec(memory_space=pltpu.SMEM)],
        out_specs=vmem,
        scratch_shapes=[
            pltpu.VMEM(spec.shape, BF16),
            pltpu.VMEM(inv.shape, BF16),
            *[pltpu.VMEM((3 * orders * width, LANES), F32)] * 3,
            *[pltpu.VMEM((shells * width, LANES), F32)] * 4,
            pltpu.VMEM((3 * orders * width, LANES), F32),
            *[pltpu.VMEM((lats * orders, LANES), F32)] * 3,
            pltpu.SemaphoreType.DMA((4,)),
        ],
        compiler_params=pltpu.CompilerParams(vmem_limit_bytes=60 * 2**20),
        name="partial_sums",
    )(spec, inv, legendre, degrees, orders_here)


def physical_body(
    orders, recv_ref, vort_ref, near_ref, far_ref, out_ref, *keep
):
    members, block, _ = recv_ref.shape
    shells = vort_ref.shape[1]
    lats = vort_ref.shape[2]
    points = vort_ref.shape[3]
    per_tile = LANES // orders
    tiles = lats // per_tile
    for i in range(per_tile):
        for h in range(members // per_tile):
            parts = [
                recv_ref[h * per_tile + j].astype(F32)[:, i * orders : (i + 1) * orders]
                for j in range(per_tile)
            ]
            joined = jnp.concatenate(parts, axis=1)
            for b in range(tiles):
                for c in range(3):
                    for k in range(2):
                        at = ((b * 3 + c) * 2 + k) * shells
                        to = pl.ds(c * shells * lats + b * per_tile + i, shells, stride=lats)
                        keep[k * (members // per_tile) + h][to, :] = joined[at : at + shells]
    left = jnp.concatenate([r[...].astype(BF16) for r in keep], axis=1)
    flat = shells * lats
    for q in range(points // LANES):
        on = slice(q * LANES, (q + 1) * LANES)
        fc, fs = far_ref[0, :, q : q + 1], far_ref[1, :, q : q + 1]
        nc, ns = near_ref[0], near_ref[1]
        trig = jnp.concatenate([nc * fc - ns * fs, -(ns * fc + nc * fs)], axis=0).astype(BF16)
        v = nn(left, trig)
        v0, v1, v2 = v[:flat], v[flat : 2 * flat], v[2 * flat :]
        w0, w1, w2 = [vort_ref[c, :, :, on].reshape(flat, LANES).astype(F32) for c in range(3)]
        shape = (shells, lats, LANES)
        out_ref[0, :, :, on] = (v1 * w2 - v2 * w1).astype(BF16).reshape(shape)
        out_ref[1, :, :, on] = (v2 * w0 - v0 * w2).astype(BF16).reshape(shape)
        out_ref[2, :, :, on] = (v0 * w1 - v1 * w0).astype(BF16).reshape(shape)


def physical(received, vorticity, near, far, orders):
    members = received.shape[0]
    _, shells, lats, _ = vorticity.shape
    vmem = pl.BlockSpec(memory_space=pltpu.VMEM)
    return pl.pallas_call(
        functools.partial(physical_body, orders),
        out_shape=jax.ShapeDtypeStruct(vorticity.shape, BF16),
        in_specs=[vmem] * 4,
        out_specs=vmem,
        scratch_shapes=[pltpu.VMEM((3 * shells * lats, LANES), F32)]
        * (2 * members * orders // LANES),
        compiler_params=pltpu.CompilerParams(vmem_limit_bytes=40 * 2**20),
        name="physical",
    )(received, vorticity, near, far)


def trig_tables(order_map, count):
    def angle(p):
        phase = order_map[:, None] * p[None, :] % count
        return phase.astype(F32) * (2.0 * math.pi / count)

    weight = jnp.where(order_map == 0, 1.0, 2.0).astype(F32)[:, None]
    near = angle(jnp.arange(LANES, dtype=jnp.int32))
    far = angle(jnp.arange(LANES, dtype=jnp.int32) * LANES)
    return (
        jnp.stack([weight * jnp.cos(near), weight * jnp.sin(near)]),
        jnp.stack([jnp.cos(far), jnp.sin(far)]),
    )


def shards(groups, members, spectral, inverse, legendre, vorticity, degree_list, order_map):
    width = spectral.shape[0]
    orders = spectral.shape[3]
    spec = jnp.transpose(spectral, (1, 2, 3, 4, 0))
    inv = jnp.transpose(inverse, (1, 2, 0))
    vort = jnp.transpose(vorticity, (0, 2, 1, 3))
    degrees = lax.dynamic_slice_in_dim(degree_list, lax.axis_index("grp") * width, width)
    orders_here = lax.dynamic_slice_in_dim(order_map, lax.axis_index("mem") * orders, orders)
    near, far = trig_tables(order_map, vorticity.shape[3])
    partial = synthesize(
        spec, inv, legendre, degrees.reshape(1, width), orders_here, groups, members
    )
    summed = lax.psum_scatter(partial, "grp", scatter_dimension=1, tiled=False)
    received = lax.all_to_all(summed, "mem", split_axis=0, concat_axis=0, tiled=True)
    out = physical(received, vort, near, far, orders)
    return jnp.transpose(out, (0, 2, 1, 3))


def solution(mesh):
    groups, members = mesh.shape["grp"], mesh.shape["mem"]

    def local(spectral, inverse, legendre, vorticity, degree_list, order_map):
        args = (spectral, inverse, legendre, vorticity, degree_list, order_map)
        width, _, _, orders, radii = spectral.shape
        shells, lats = inverse.shape[1], legendre.shape[1]
        fits = (
            width == LANES
            and 2 * shells <= LANES
            and LANES < radii
            and 2 * radii == 3 * LANES
            and LANES % orders == 0
            and (shells // groups * 2) % 8 == 0
            and members % (LANES // orders) == 0
            and (lats // members) % (LANES // orders) == 0
            and vorticity.shape[3] % LANES == 0
            and vorticity.shape[3] // LANES <= LANES
        )
        if fits:
            return shards(groups, members, *args)
        return plain_shards(*args)

    return jax.shard_map(
        local,
        mesh=mesh,
        in_specs=(
            P("grp", None, None, "mem", None),
            P("grp", None, None),
            P("mem", None, "grp"),
            P(None, "mem", "grp", None),
            P(),
            P(),
        ),
        out_specs=P(None, "mem", "grp", None),
        check_vma=False,
    )
```

```python
import functools
import math

import jax
import jax.numpy as jnp
from jax import lax
from jax.experimental import pallas as pl
from jax.experimental.pallas import tpu as pltpu
from jax.sharding import PartitionSpec as P

F32 = jnp.float32
BF16 = jnp.bfloat16
LANES = 128
NT = (((1,), (1,)), ((), ()))
NN = (((1,), (0,)), ((), ()))


def nt(a, b):
    return lax.dot_general(a, b, NT, preferred_element_type=F32)


def nn(a, b):
    return lax.dot_general(a, b, NN, preferred_element_type=F32)


def cross_product(flow_velocity, vorticity):
    other = vorticity.astype(jnp.float32)
    first = flow_velocity[:, :, 1] * other[2] - flow_velocity[:, :, 2] * other[1]
    second = flow_velocity[:, :, 2] * other[0] - flow_velocity[:, :, 0] * other[2]
    third = flow_velocity[:, :, 0] * other[1] - flow_velocity[:, :, 1] * other[0]
    return jnp.stack([first, second, third]).astype(jnp.bfloat16)


def fourier_table(order_map, count):
    longitude = jnp.arange(count, dtype=jnp.int32)
    phase = order_map[:, None] * longitude[None, :] % count
    angle = phase.astype(jnp.float32) * (2.0 * math.pi / count)
    weight = jnp.where(order_map == 0, 1.0, 2.0).astype(jnp.float32)[:, None]
    return jnp.stack([weight * jnp.cos(angle), -weight * jnp.sin(angle)], axis=1).astype(
        jnp.bfloat16
    )


def plain_shards(spectral, inverse, legendre, vorticity, degree_list, order_map):
    orders = spectral.shape[3]
    shells = vorticity.shape[2]
    local_order_list = lax.dynamic_slice_in_dim(
        order_map, lax.axis_index("mem") * orders, orders
    )
    width = spectral.shape[0]
    flat = spectral.reshape(width, 6 * orders, spectral.shape[4])
    solved = lax.dot_general(
        inverse, flat, (((2,), (2,)), ((0,), (0,))), preferred_element_type=F32
    ).astype(BF16)
    moved = lax.all_to_all(solved, "grp", split_axis=1, concat_axis=0, tiled=True)
    by_order = jnp.transpose(
        moved.reshape(moved.shape[0], moved.shape[1] * 6, orders), (2, 0, 1)
    )
    segment = lax.all_gather(legendre, "grp", axis=2, tiled=True)
    allowed = local_order_list[:, None] <= degree_list[None, :]
    table = jnp.where(allowed[:, None, :], segment, jnp.zeros_like(segment))
    latitudinal = lax.dot_general(
        table, by_order, (((2,), (1,)), ((0,), (0,))), preferred_element_type=F32
    ).astype(BF16)
    gathered = lax.all_to_all(latitudinal, "mem", split_axis=1, concat_axis=0, tiled=True)
    arranged = gathered.reshape(gathered.shape[0], gathered.shape[1], shells, 3, 2)
    trig = fourier_table(order_map, vorticity.shape[3])
    velocity = jnp.einsum("mtsck,mkp->tscp", arranged, trig, preferred_element_type=F32)
    return cross_product(velocity, vorticity)


def synth_body(
    groups, members, spec_hbm, inv_hbm, leg_ref, deg_ref, ord_ref, send_ref,
    spec, inv, t0, t1, t2, i0, i1, i2, i3, solved, f0, f1, f2, sems,
):
    orders, radii, width = spec.shape[2:]
    shells = inv.shape[0]
    lats = leg_ref.shape[1]
    half = LANES // 2
    fill = 2 * LANES - radii
    rows = 3 * orders
    mine = shells // groups
    per_tile = LANES // orders
    pitch, lat_pitch = width + 1, orders + 1

    inv_copy = pltpu.make_async_copy(inv_hbm, inv, sems.at[3])
    inv_copy.start()
    copies = [pltpu.make_async_copy(spec_hbm.at[c], spec.at[c], sems.at[c]) for c in range(3)]
    for copy in copies:
        copy.start()

    eye = (
        lax.broadcasted_iota(jnp.int32, (width, width), 0)
        == lax.broadcasted_iota(jnp.int32, (width, width), 1)
    ).astype(BF16)
    gap = jnp.zeros((fill, width), BF16)

    inv_copy.wait()

    def turn_inverse(s, carry):
        a = inv[s]
        out = nt(eye, jnp.concatenate([a, gap, gap, a], axis=0))
        at = pl.ds(s * pitch, width)
        i0[at, :] = out[:, 0:LANES]
        i1[at, :] = out[:, LANES : 2 * LANES]
        i2[at, :] = out[:, 2 * LANES : 3 * LANES]
        i3[at, :] = out[:, 3 * LANES : 4 * LANES]
        return carry

    lax.fori_loop(0, shells, turn_inverse, 0, unroll=4)

    for c in range(3):
        copies[c].wait()

        def turn_profiles(m, carry):
            out = nt(eye, jnp.concatenate([spec[c, 0, m], spec[c, 1, m]], axis=0))
            at = pl.ds((c * orders + m) * pitch, width)
            t0[at, :] = out[:, 0:LANES]
            t1[at, :] = out[:, LANES : 2 * LANES]
            t2[at, :] = out[:, 2 * LANES : 3 * LANES]
            return carry

        lax.fori_loop(0, orders, turn_profiles, 0, unroll=4)

    nothing = jnp.zeros((shells, LANES), BF16)
    pad = jnp.zeros((half - shells, 3 * LANES), BF16)

    def solve(l, carry):
        at = pl.ds(l, rows, stride=pitch)
        profiles = jnp.concatenate([r[at, :].astype(BF16) for r in (t0, t1, t2)], axis=1)
        on = pl.ds(l, shells, stride=pitch)
        real = jnp.concatenate([i0[on, :].astype(BF16), i1[on, :].astype(BF16), nothing], axis=1)
        imag = jnp.concatenate([nothing, i2[on, :].astype(BF16), i3[on, :].astype(BF16)], axis=1)
        solved[at, :] = nt(profiles, jnp.concatenate([real, pad, imag, pad], axis=0))
        return carry

    lax.fori_loop(0, width, solve, 0, unroll=4)

    degrees = deg_ref[...]

    def sum_degrees(m, carry):
        table = jnp.where(degrees >= ord_ref[m], leg_ref[m].astype(F32), 0.0).astype(BF16)
        block = jnp.concatenate(
            [
                solved[pl.ds((c * orders + m) * pitch, width), :].astype(BF16)
                for c in range(3)
            ],
            axis=1,
        )
        out = nn(table, block)
        at = pl.ds(m, lats, stride=lat_pitch)
        f0[at, :] = out[:, 0:LANES]
        f1[at, :] = out[:, LANES : 2 * LANES]
        f2[at, :] = out[:, 2 * LANES : 3 * LANES]
        return carry

    lax.fori_loop(0, orders, sum_degrees, 0, unroll=4)

    row = lax.broadcasted_iota(jnp.int32, (2 * shells, LANES), 0)
    lane = lax.broadcasted_iota(jnp.int32, (2 * shells, LANES), 1)
    want = row
    for i in range(1, 2 * groups):
        g, k = i // 2, i % 2
        step = (half + g * mine - i * mine) if k else (g * mine - i * mine)
        want = jnp.where(row >= i * mine, row + step, want)
    pick = (want == lane).astype(BF16)
    tiles = lats // members // per_tile

    def turn_sums(j, carry):
        parts = []
        for b in range(tiles):
            at = [
                pl.ds(((j * tiles + b) * per_tile + i) * lat_pitch, orders)
                for i in range(per_tile)
            ]
            for f in (f0, f1, f2):
                both = jnp.concatenate([f[a, :].astype(BF16) for a in at], axis=0)
                parts.append(nt(pick, both))
        for g in range(groups):
            block = [p[g * 2 * mine : (g + 1) * 2 * mine] for p in parts]
            send_ref[j, g % 2, g // 2] = jnp.concatenate(block, axis=0).astype(BF16)
        return carry

    lax.fori_loop(0, members, turn_sums, 0)


def synthesize(spec, inv, legendre, degrees, orders_here, groups, members):
    _, _, orders, radii, width = spec.shape
    shells = inv.shape[0]
    lats = legendre.shape[1]
    mine = shells // groups
    block = lats // members * orders * mine * 6 // LANES
    pitch = width + 1
    any_space = pl.BlockSpec(memory_space=pl.ANY)
    vmem = pl.BlockSpec(memory_space=pltpu.VMEM)
    return pl.pallas_call(
        functools.partial(synth_body, groups, members),
        out_shape=jax.ShapeDtypeStruct((members, 2, groups // 2, block, LANES), BF16),
        in_specs=[any_space, any_space, vmem, vmem, pl.BlockSpec(memory_space=pltpu.SMEM)],
        out_specs=vmem,
        scratch_shapes=[
            pltpu.VMEM(spec.shape, BF16),
            pltpu.VMEM(inv.shape, BF16),
            *[pltpu.VMEM((3 * orders * pitch, LANES), F32)] * 3,
            *[pltpu.VMEM((shells * pitch, LANES), F32)] * 4,
            pltpu.VMEM((3 * orders * pitch, LANES), F32),
            *[pltpu.VMEM((lats * (orders + 1), LANES), F32)] * 3,
            pltpu.SemaphoreType.DMA((4,)),
        ],
        compiler_params=pltpu.CompilerParams(vmem_limit_bytes=60 * 2**20),
        name="partial_sums",
    )(spec, inv, legendre, degrees, orders_here)


MESH = pl.DeviceIdType.MESH


def exchange_body(
    send_ref, out_ref, from_sib, to_far, from_far, to_mem, recv,
    sib_s, sib_r, far_s, far_r, mem_s, mem_r,
):
    members = send_ref.shape[0]
    grp, me = lax.axis_index("grp"), lax.axis_index("mem")
    y, core = grp // 2, grp % 2
    sibling = y * 2 + (1 - core)
    across = (1 - y) * 2 + core

    barrier = pltpu.get_barrier_semaphore()
    for g in (sibling, across):
        pl.semaphore_signal(barrier, inc=1, device_id=(g, me), device_id_type=MESH)
    for i in range(1, members):
        pl.semaphore_signal(
            barrier, inc=1, device_id=(grp, (me + i) % members), device_id_type=MESH
        )
    pl.semaphore_wait(barrier, members + 1)

    def to_sibling(j):
        return pltpu.make_async_remote_copy(
            src_ref=send_ref.at[j, 1 - core], dst_ref=from_sib.at[j],
            send_sem=sib_s.at[j], recv_sem=sib_r.at[j],
            device_id=(sibling, me), device_id_type=MESH,
        )

    def to_across(j):
        return pltpu.make_async_remote_copy(
            src_ref=to_far.at[j], dst_ref=from_far.at[j],
            send_sem=far_s.at[j], recv_sem=far_r.at[j],
            device_id=(across, me), device_id_type=MESH,
        )

    def to_member(j, slot):
        return pltpu.make_async_remote_copy(
            src_ref=to_mem.at[j], dst_ref=recv.at[slot],
            send_sem=mem_s.at[j], recv_sem=mem_r.at[slot],
            device_id=(grp, j), device_id_type=MESH,
        )

    def target(i):
        return (me + 1 + i) % members

    def start(i, carry):
        to_sibling(target(i)).start()
        return carry

    lax.fori_loop(0, members, start, 0)

    def pair_sum(j, half):
        return send_ref[j, core, half].astype(F32) + from_sib[j, half].astype(F32)

    def second(i, carry):
        j = target(i)
        to_sibling(j).wait_recv()
        to_far[j] = pair_sum(j, 1 - y).astype(BF16)
        to_across(j).start()
        return carry

    lax.fori_loop(0, members, second, 0)

    def total(j):
        to_across(j).wait_recv()
        return (pair_sum(j, y) + from_far[j].astype(F32)).astype(BF16)

    def third(i, carry):
        j = target(i)
        to_mem[j] = total(j)
        to_member(j, me).start()
        return carry

    lax.fori_loop(0, members - 1, third, 0)
    out_ref[me] = total(me)

    def finish(i, carry):
        j = target(i)
        to_member(j, j).wait_recv()
        out_ref[j] = recv[j]
        return carry

    lax.fori_loop(0, members - 1, finish, 0)

    def drain(i, carry):
        j = target(i)
        to_sibling(j).wait_send()
        to_across(j).wait_send()
        return carry

    lax.fori_loop(0, members, drain, 0)

    def drain_members(i, carry):
        to_member(target(i), me).wait_send()
        return carry

    lax.fori_loop(0, members - 1, drain_members, 0)


def exchange(partial):
    members, cores, far, block, _ = partial.shape
    vmem = pl.BlockSpec(memory_space=pltpu.VMEM)
    slots = pltpu.VMEM((members, block, LANES), BF16)
    return pl.pallas_call(
        exchange_body,
        out_shape=jax.ShapeDtypeStruct((members, block, LANES), BF16),
        in_specs=[vmem],
        out_specs=vmem,
        scratch_shapes=[
            pltpu.VMEM((members, far, block, LANES), BF16),
            slots, slots, slots, slots,
            *[pltpu.SemaphoreType.DMA((members,))] * 6,
        ],
        compiler_params=pltpu.CompilerParams(
            collective_id=0, has_side_effects=True, vmem_limit_bytes=32 * 2**20
        ),
        name="exchange",
    )(partial)


def physical_body(
    orders, recv_ref, vort_ref, near_ref, far_ref, out_ref, *keep
):
    members, block, _ = recv_ref.shape
    shells = vort_ref.shape[1]
    lats = vort_ref.shape[2]
    points = vort_ref.shape[3]
    per_tile = LANES // orders
    tiles = lats // per_tile
    for i in range(per_tile):
        for h in range(members // per_tile):
            parts = [
                recv_ref[h * per_tile + j].astype(F32)[:, i * orders : (i + 1) * orders]
                for j in range(per_tile)
            ]
            joined = jnp.concatenate(parts, axis=1)
            for b in range(tiles):
                for c in range(3):
                    for k in range(2):
                        at = ((b * 3 + c) * 2 + k) * shells
                        to = pl.ds(c * shells * lats + b * per_tile + i, shells, stride=lats)
                        keep[k * (members // per_tile) + h][to, :] = joined[at : at + shells]
    left = jnp.concatenate([r[...].astype(BF16) for r in keep], axis=1)
    flat = shells * lats
    for q in range(points // LANES):
        on = slice(q * LANES, (q + 1) * LANES)
        fc, fs = far_ref[0, :, q : q + 1], far_ref[1, :, q : q + 1]
        nc, ns = near_ref[0], near_ref[1]
        trig = jnp.concatenate([nc * fc - ns * fs, -(ns * fc + nc * fs)], axis=0).astype(BF16)
        v = nn(left, trig)
        v0, v1, v2 = v[:flat], v[flat : 2 * flat], v[2 * flat :]
        w0, w1, w2 = [vort_ref[c, :, :, on].reshape(flat, LANES).astype(F32) for c in range(3)]
        shape = (shells, lats, LANES)
        out_ref[0, :, :, on] = (v1 * w2 - v2 * w1).astype(BF16).reshape(shape)
        out_ref[1, :, :, on] = (v2 * w0 - v0 * w2).astype(BF16).reshape(shape)
        out_ref[2, :, :, on] = (v0 * w1 - v1 * w0).astype(BF16).reshape(shape)


def physical(received, vorticity, near, far, orders):
    members = received.shape[0]
    _, shells, lats, _ = vorticity.shape
    vmem = pl.BlockSpec(memory_space=pltpu.VMEM)
    return pl.pallas_call(
        functools.partial(physical_body, orders),
        out_shape=jax.ShapeDtypeStruct(vorticity.shape, BF16),
        in_specs=[vmem] * 4,
        out_specs=vmem,
        scratch_shapes=[pltpu.VMEM((3 * shells * lats, LANES), F32)]
        * (2 * members * orders // LANES),
        compiler_params=pltpu.CompilerParams(vmem_limit_bytes=40 * 2**20),
        name="physical",
    )(received, vorticity, near, far)


def trig_tables(order_map, count):
    def angle(p):
        phase = order_map[:, None] * p[None, :] % count
        return phase.astype(F32) * (2.0 * math.pi / count)

    weight = jnp.where(order_map == 0, 1.0, 2.0).astype(F32)[:, None]
    near = angle(jnp.arange(LANES, dtype=jnp.int32))
    far = angle(jnp.arange(LANES, dtype=jnp.int32) * LANES)
    return (
        jnp.stack([weight * jnp.cos(near), weight * jnp.sin(near)]),
        jnp.stack([jnp.cos(far), jnp.sin(far)]),
    )


def shards(groups, members, spectral, inverse, legendre, vorticity, degree_list, order_map):
    width = spectral.shape[0]
    orders = spectral.shape[3]
    spec = jnp.transpose(spectral, (1, 2, 3, 4, 0))
    inv = jnp.transpose(inverse, (1, 2, 0))
    vort = jnp.transpose(vorticity, (0, 2, 1, 3))
    degrees = lax.dynamic_slice_in_dim(degree_list, lax.axis_index("grp") * width, width)
    orders_here = lax.dynamic_slice_in_dim(order_map, lax.axis_index("mem") * orders, orders)
    near, far = trig_tables(order_map, vorticity.shape[3])
    partial = synthesize(
        spec, inv, legendre, degrees.reshape(1, width), orders_here, groups, members
    )
    received = exchange(partial)
    out = physical(received, vort, near, far, orders)
    return jnp.transpose(out, (0, 2, 1, 3))


def solution(mesh):
    groups, members = mesh.shape["grp"], mesh.shape["mem"]

    def local(spectral, inverse, legendre, vorticity, degree_list, order_map):
        args = (spectral, inverse, legendre, vorticity, degree_list, order_map)
        width, _, _, orders, radii = spectral.shape
        shells, lats = inverse.shape[1], legendre.shape[1]
        fits = (
            groups == 4
            and width == LANES
            and 2 * shells <= LANES
            and LANES < radii
            and 2 * radii == 3 * LANES
            and LANES % orders == 0
            and (shells // groups * 2) % 8 == 0
            and members % (LANES // orders) == 0
            and (lats // members) % (LANES // orders) == 0
            and vorticity.shape[3] % LANES == 0
            and vorticity.shape[3] // LANES <= LANES
        )
        if fits:
            return shards(groups, members, *args)
        return plain_shards(*args)

    return jax.shard_map(
        local,
        mesh=mesh,
        in_specs=(
            P("grp", None, None, "mem", None),
            P("grp", None, None),
            P("mem", None, "grp"),
            P(None, "mem", "grp", None),
            P(),
            P(),
        ),
        out_specs=P(None, "mem", "grp", None),
        check_vma=False,
    )
```

```python
import functools
import math

import jax
import jax.numpy as jnp
from jax import lax
from jax.experimental import pallas as pl
from jax.experimental.pallas import tpu as pltpu
from jax.sharding import PartitionSpec as P

F32 = jnp.float32
BF16 = jnp.bfloat16
LANES = 128
NT = (((1,), (1,)), ((), ()))
NN = (((1,), (0,)), ((), ()))


def nt(a, b):
    return lax.dot_general(a, b, NT, preferred_element_type=F32)


def nn(a, b):
    return lax.dot_general(a, b, NN, preferred_element_type=F32)


def cross_product(flow_velocity, vorticity):
    other = vorticity.astype(jnp.float32)
    first = flow_velocity[:, :, 1] * other[2] - flow_velocity[:, :, 2] * other[1]
    second = flow_velocity[:, :, 2] * other[0] - flow_velocity[:, :, 0] * other[2]
    third = flow_velocity[:, :, 0] * other[1] - flow_velocity[:, :, 1] * other[0]
    return jnp.stack([first, second, third]).astype(jnp.bfloat16)


def fourier_table(order_map, count):
    longitude = jnp.arange(count, dtype=jnp.int32)
    phase = order_map[:, None] * longitude[None, :] % count
    angle = phase.astype(jnp.float32) * (2.0 * math.pi / count)
    weight = jnp.where(order_map == 0, 1.0, 2.0).astype(jnp.float32)[:, None]
    return jnp.stack([weight * jnp.cos(angle), -weight * jnp.sin(angle)], axis=1).astype(
        jnp.bfloat16
    )


def plain_shards(spectral, inverse, legendre, vorticity, degree_list, order_map):
    orders = spectral.shape[3]
    shells = vorticity.shape[2]
    local_order_list = lax.dynamic_slice_in_dim(
        order_map, lax.axis_index("mem") * orders, orders
    )
    width = spectral.shape[0]
    flat = spectral.reshape(width, 6 * orders, spectral.shape[4])
    solved = lax.dot_general(
        inverse, flat, (((2,), (2,)), ((0,), (0,))), preferred_element_type=F32
    ).astype(BF16)
    moved = lax.all_to_all(solved, "grp", split_axis=1, concat_axis=0, tiled=True)
    by_order = jnp.transpose(
        moved.reshape(moved.shape[0], moved.shape[1] * 6, orders), (2, 0, 1)
    )
    segment = lax.all_gather(legendre, "grp", axis=2, tiled=True)
    allowed = local_order_list[:, None] <= degree_list[None, :]
    table = jnp.where(allowed[:, None, :], segment, jnp.zeros_like(segment))
    latitudinal = lax.dot_general(
        table, by_order, (((2,), (1,)), ((0,), (0,))), preferred_element_type=F32
    ).astype(BF16)
    gathered = lax.all_to_all(latitudinal, "mem", split_axis=1, concat_axis=0, tiled=True)
    arranged = gathered.reshape(gathered.shape[0], gathered.shape[1], shells, 3, 2)
    trig = fourier_table(order_map, vorticity.shape[3])
    velocity = jnp.einsum("mtsck,mkp->tscp", arranged, trig, preferred_element_type=F32)
    return cross_product(velocity, vorticity)


def synth_body(
    groups, members, spec_hbm, inv_hbm, leg_ref, deg_ref, ord_ref, send_ref,
    spec, inv, t0, t1, t2, main, rest, solved, f0, f1, f2, sems,
):
    orders, radii, width = spec.shape[2:]
    shells = inv.shape[0]
    lats = leg_ref.shape[1]
    half = LANES // 2
    rows = 3 * orders
    mine = shells // groups
    per_tile = LANES // orders
    pitch, lat_pitch = width + 1, orders + 1

    inv_copy = pltpu.make_async_copy(inv_hbm, inv, sems.at[3])
    inv_copy.start()
    copies = [pltpu.make_async_copy(spec_hbm.at[c], spec.at[c], sems.at[c]) for c in range(3)]
    for copy in copies:
        copy.start()

    eye = (
        lax.broadcasted_iota(jnp.int32, (2 * width, 2 * width), 0)
        == lax.broadcasted_iota(jnp.int32, (2 * width, 2 * width), 1)
    ).astype(BF16)

    inv_copy.wait()

    def turn_inverse(i, carry):
        both = jnp.concatenate([inv[2 * i], inv[2 * i + 1]], axis=1)
        out = nt(eye, jnp.concatenate([both, both[LANES:]], axis=0))
        for h in range(2):
            at = pl.ds((2 * i + h) * pitch, width)
            part = out[h * width : (h + 1) * width]
            main[at, :] = part[:, 0:LANES]
            rest[at, :] = part[:, LANES : 2 * LANES]
        return carry

    lax.fori_loop(0, shells // 2, turn_inverse, 0, unroll=4)

    for c in range(3):
        copies[c].wait()

        def turn_profiles(i, carry):
            a, b = [
                jnp.concatenate([spec[c, k, 2 * i], spec[c, k, 2 * i + 1]], axis=1)
                for k in range(2)
            ]
            out = nt(eye, jnp.concatenate([a, b[LANES:], b[:LANES]], axis=0))
            for h in range(2):
                at = pl.ds((c * orders + 2 * i + h) * pitch, width)
                part = out[h * width : (h + 1) * width]
                t0[at, :] = part[:, 0:LANES]
                t1[at, :] = part[:, LANES : 2 * LANES]
                t2[at, :] = part[:, 2 * LANES : 3 * LANES]
            return carry

        lax.fori_loop(0, orders // 2, turn_profiles, 0, unroll=4)

    nothing = jnp.zeros((shells, LANES), BF16)
    pad = jnp.zeros((half - shells, 3 * LANES), BF16)
    low = lax.broadcasted_iota(jnp.int32, (shells, LANES), 1) < half

    def solve(l, carry):
        at = pl.ds(l, rows, stride=pitch)
        profiles = jnp.concatenate([r[at, :].astype(BF16) for r in (t0, t1, t2)], axis=1)
        on = pl.ds(l, shells, stride=pitch)
        first, last = main[on, :].astype(BF16), rest[on, :]
        lower = jnp.where(low, last, 0.0).astype(BF16)
        upper = jnp.where(low, 0.0, last).astype(BF16)
        real = jnp.concatenate([first, lower, nothing], axis=1)
        imag = jnp.concatenate([nothing, upper, first], axis=1)
        solved[at, :] = nt(profiles, jnp.concatenate([real, pad, imag, pad], axis=0))
        return carry

    lax.fori_loop(0, width, solve, 0, unroll=16)

    start = pl.multiple_of(lax.axis_index("grp") * width, width)
    degrees = deg_ref[pl.ds(start, width)].reshape(1, width)
    first_order = lax.axis_index("mem") * orders

    def sum_degrees(m, carry):
        valid = degrees >= ord_ref[first_order + m]
        table = jnp.where(valid, leg_ref[m].astype(F32), 0.0).astype(BF16)
        block = jnp.concatenate(
            [
                solved[pl.ds((c * orders + m) * pitch, width), :].astype(BF16)
                for c in range(3)
            ],
            axis=1,
        )
        out = nn(table, block)
        at = pl.ds(m, lats, stride=lat_pitch)
        f0[at, :] = out[:, 0:LANES]
        f1[at, :] = out[:, LANES : 2 * LANES]
        f2[at, :] = out[:, 2 * LANES : 3 * LANES]
        return carry

    lax.fori_loop(0, orders, sum_degrees, 0, unroll=8)

    row = lax.broadcasted_iota(jnp.int32, (2 * shells, LANES), 0)
    lane = lax.broadcasted_iota(jnp.int32, (2 * shells, LANES), 1)
    want = row
    for i in range(1, 2 * groups):
        g, k = i // 2, i % 2
        step = (half + g * mine - i * mine) if k else (g * mine - i * mine)
        want = jnp.where(row >= i * mine, row + step, want)
    pick = (want == lane).astype(BF16)
    tiles = lats // members // per_tile

    def turn_sums(j, carry):
        parts = []
        for b in range(tiles):
            at = [
                pl.ds(((j * tiles + b) * per_tile + i) * lat_pitch, orders)
                for i in range(per_tile)
            ]
            for f in (f0, f1, f2):
                both = jnp.concatenate([f[a, :].astype(BF16) for a in at], axis=0)
                parts.append(nt(pick, both))
        for g in range(groups):
            block = [p[g * 2 * mine : (g + 1) * 2 * mine] for p in parts]
            send_ref[j, g % 2, g // 2] = jnp.concatenate(block, axis=0).astype(BF16)
        return carry

    lax.fori_loop(0, members, turn_sums, 0, unroll=2)


def synthesize(spec, inv, legendre, degree_list, order_map, groups, members):
    _, _, orders, radii, width = spec.shape
    shells = inv.shape[0]
    lats = legendre.shape[1]
    mine = shells // groups
    block = lats // members * orders * mine * 6 // LANES
    pitch = width + 1
    any_space = pl.BlockSpec(memory_space=pl.ANY)
    vmem = pl.BlockSpec(memory_space=pltpu.VMEM)
    return pl.pallas_call(
        functools.partial(synth_body, groups, members),
        out_shape=jax.ShapeDtypeStruct((members, 2, groups // 2, block, LANES), BF16),
        in_specs=[any_space, any_space, vmem, vmem, pl.BlockSpec(memory_space=pltpu.SMEM)],
        out_specs=vmem,
        scratch_shapes=[
            pltpu.VMEM(spec.shape, BF16),
            pltpu.VMEM(inv.shape, BF16),
            *[pltpu.VMEM((3 * orders * pitch, LANES), F32)] * 3,
            *[pltpu.VMEM((shells * pitch, LANES), F32)] * 2,
            pltpu.VMEM((3 * orders * pitch, LANES), F32),
            *[pltpu.VMEM((lats * (orders + 1), LANES), F32)] * 3,
            pltpu.SemaphoreType.DMA((4,)),
        ],
        compiler_params=pltpu.CompilerParams(vmem_limit_bytes=60 * 2**20),
        name="partial_sums",
    )(spec, inv, legendre, degree_list, order_map)


MESH = pl.DeviceIdType.MESH


def exchange_body(
    send_ref, out_ref, from_sib, to_far, from_far, to_mem, recv,
    sib_s, sib_r, far_s, far_r, mem_s, mem_r,
):
    members = send_ref.shape[0]
    grp, me = lax.axis_index("grp"), lax.axis_index("mem")
    y, core = grp // 2, grp % 2
    sibling = y * 2 + (1 - core)
    across = (1 - y) * 2 + core

    barrier = pltpu.get_barrier_semaphore()
    for g in (sibling, across):
        pl.semaphore_signal(barrier, inc=1, device_id=(g, me), device_id_type=MESH)
    for i in range(1, members):
        pl.semaphore_signal(
            barrier, inc=1, device_id=(grp, (me + i) % members), device_id_type=MESH
        )
    pl.semaphore_wait(barrier, members + 1)

    def to_sibling(j):
        return pltpu.make_async_remote_copy(
            src_ref=send_ref.at[j, 1 - core], dst_ref=from_sib.at[j],
            send_sem=sib_s.at[j], recv_sem=sib_r.at[j],
            device_id=(sibling, me), device_id_type=MESH,
        )

    def to_across(j):
        return pltpu.make_async_remote_copy(
            src_ref=to_far.at[j], dst_ref=from_far.at[j],
            send_sem=far_s.at[j], recv_sem=far_r.at[j],
            device_id=(across, me), device_id_type=MESH,
        )

    def to_member(j, slot):
        return pltpu.make_async_remote_copy(
            src_ref=to_mem.at[j], dst_ref=recv.at[slot],
            send_sem=mem_s.at[j], recv_sem=mem_r.at[slot],
            device_id=(grp, j), device_id_type=MESH,
        )

    def target(i):
        return (me + 1 + i) % members

    def start(i, carry):
        to_sibling(target(i)).start()
        return carry

    lax.fori_loop(0, members, start, 0)

    def pair_sum(j, half):
        return send_ref[j, core, half].astype(F32) + from_sib[j, half].astype(F32)

    def second(i, carry):
        j = target(i)
        to_sibling(j).wait_recv()
        to_far[j] = pair_sum(j, 1 - y).astype(BF16)
        to_across(j).start()
        return carry

    lax.fori_loop(0, members, second, 0)

    def total(j):
        to_across(j).wait_recv()
        return (pair_sum(j, y) + from_far[j].astype(F32)).astype(BF16)

    def third(i, carry):
        j = target(i)
        to_mem[j] = total(j)
        to_member(j, me).start()
        return carry

    lax.fori_loop(0, members - 1, third, 0)
    out_ref[me] = total(me)

    def finish(i, carry):
        j = target(i)
        to_member(j, j).wait_recv()
        out_ref[j] = recv[j]
        return carry

    lax.fori_loop(0, members - 1, finish, 0)

    def drain(i, carry):
        j = target(i)
        to_sibling(j).wait_send()
        to_across(j).wait_send()
        return carry

    lax.fori_loop(0, members, drain, 0)

    def drain_members(i, carry):
        to_member(target(i), me).wait_send()
        return carry

    lax.fori_loop(0, members - 1, drain_members, 0)


def exchange(partial):
    members, cores, far, block, _ = partial.shape
    vmem = pl.BlockSpec(memory_space=pltpu.VMEM)
    slots = pltpu.VMEM((members, block, LANES), BF16)
    return pl.pallas_call(
        exchange_body,
        out_shape=jax.ShapeDtypeStruct((members, block, LANES), BF16),
        in_specs=[vmem],
        out_specs=vmem,
        scratch_shapes=[
            pltpu.VMEM((members, far, block, LANES), BF16),
            slots, slots, slots, slots,
            *[pltpu.SemaphoreType.DMA((members,))] * 6,
        ],
        compiler_params=pltpu.CompilerParams(
            collective_id=0, has_side_effects=True, vmem_limit_bytes=32 * 2**20
        ),
        name="exchange",
    )(partial)


def physical_body(
    orders, recv_ref, vort_hbm, near_ref, far_ref, out_ref, vort_ref, sem, *keep
):
    copy = pltpu.make_async_copy(vort_hbm, vort_ref, sem.at[0])
    copy.start()
    members, block, _ = recv_ref.shape
    shells = vort_ref.shape[1]
    lats = vort_ref.shape[2]
    points = vort_ref.shape[3]
    per_tile = LANES // orders
    tiles = lats // per_tile
    for i in range(per_tile):
        for h in range(members // per_tile):
            parts = [
                recv_ref[h * per_tile + j].astype(F32)[:, i * orders : (i + 1) * orders]
                for j in range(per_tile)
            ]
            joined = jnp.concatenate(parts, axis=1)
            for b in range(tiles):
                for c in range(3):
                    for k in range(2):
                        at = ((b * 3 + c) * 2 + k) * shells
                        to = pl.ds(c * shells * lats + b * per_tile + i, shells, stride=lats)
                        keep[k * (members // per_tile) + h][to, :] = joined[at : at + shells]
    left = jnp.concatenate([r[...].astype(BF16) for r in keep], axis=1)
    flat = shells * lats
    copy.wait()
    for q in range(points // LANES):
        on = slice(q * LANES, (q + 1) * LANES)
        fc, fs = far_ref[0, :, q : q + 1], far_ref[1, :, q : q + 1]
        nc, ns = near_ref[0], near_ref[1]
        trig = jnp.concatenate([nc * fc - ns * fs, -(ns * fc + nc * fs)], axis=0).astype(BF16)
        v = nn(left, trig)
        v0, v1, v2 = v[:flat], v[flat : 2 * flat], v[2 * flat :]
        w0, w1, w2 = [vort_ref[c, :, :, on].reshape(flat, LANES).astype(F32) for c in range(3)]
        shape = (shells, lats, LANES)
        out_ref[0, :, :, on] = (v1 * w2 - v2 * w1).astype(BF16).reshape(shape)
        out_ref[1, :, :, on] = (v2 * w0 - v0 * w2).astype(BF16).reshape(shape)
        out_ref[2, :, :, on] = (v0 * w1 - v1 * w0).astype(BF16).reshape(shape)


def physical(received, vorticity, near, far, orders):
    members = received.shape[0]
    _, shells, lats, _ = vorticity.shape
    vmem = pl.BlockSpec(memory_space=pltpu.VMEM)
    return pl.pallas_call(
        functools.partial(physical_body, orders),
        out_shape=jax.ShapeDtypeStruct(vorticity.shape, BF16),
        in_specs=[vmem, pl.BlockSpec(memory_space=pl.ANY), vmem, vmem],
        out_specs=vmem,
        scratch_shapes=[pltpu.VMEM(vorticity.shape, BF16), pltpu.SemaphoreType.DMA((1,))]
        + [pltpu.VMEM((3 * shells * lats, LANES), F32)] * (2 * members * orders // LANES),
        compiler_params=pltpu.CompilerParams(vmem_limit_bytes=40 * 2**20),
        name="physical",
    )(received, vorticity, near, far)


def trig_tables(order_map, count):
    def angle(p):
        phase = order_map[:, None] * p[None, :] % count
        return phase.astype(F32) * (2.0 * math.pi / count)

    weight = jnp.where(order_map == 0, 1.0, 2.0).astype(F32)[:, None]
    near = angle(jnp.arange(LANES, dtype=jnp.int32))
    far = angle(jnp.arange(LANES, dtype=jnp.int32) * LANES)
    return (
        jnp.stack([weight * jnp.cos(near), weight * jnp.sin(near)]),
        jnp.stack([jnp.cos(far), jnp.sin(far)]),
    )


def shards(groups, members, spectral, inverse, legendre, vorticity, degree_list, order_map):
    orders = spectral.shape[3]
    spec = jnp.transpose(spectral, (1, 2, 3, 4, 0))
    inv = jnp.transpose(inverse, (1, 2, 0))
    vort = jnp.transpose(vorticity, (0, 2, 1, 3))
    near, far = trig_tables(order_map, vorticity.shape[3])
    partial = synthesize(spec, inv, legendre, degree_list, order_map, groups, members)
    received = exchange(partial)
    out = physical(received, vort, near, far, orders)
    return jnp.transpose(out, (0, 2, 1, 3))


def solution(mesh):
    groups, members = mesh.shape["grp"], mesh.shape["mem"]

    def local(spectral, inverse, legendre, vorticity, degree_list, order_map):
        args = (spectral, inverse, legendre, vorticity, degree_list, order_map)
        width, _, _, orders, radii = spectral.shape
        shells, lats = inverse.shape[1], legendre.shape[1]
        fits = (
            groups == 4
            and width == LANES
            and 2 * shells <= LANES
            and LANES < radii
            and 2 * radii == 3 * LANES
            and LANES % orders == 0
            and orders % 2 == 0
            and shells % 2 == 0
            and (shells // groups * 2) % 8 == 0
            and members % (LANES // orders) == 0
            and (lats // members) % (LANES // orders) == 0
            and vorticity.shape[3] % LANES == 0
            and vorticity.shape[3] // LANES <= LANES
        )
        if fits:
            return shards(groups, members, *args)
        return plain_shards(*args)

    return jax.shard_map(
        local,
        mesh=mesh,
        in_specs=(
            P("grp", None, None, "mem", None),
            P("grp", None, None),
            P("mem", None, "grp"),
            P(None, "mem", "grp", None),
            P(),
            P(),
        ),
        out_specs=P(None, "mem", "grp", None),
        check_vma=False,
    )
```

```python
import functools
import math

import jax
import jax.numpy as jnp
from jax import lax
from jax.experimental import pallas as pl
from jax.experimental.pallas import tpu as pltpu
from jax.sharding import PartitionSpec as P

F32 = jnp.float32
BF16 = jnp.bfloat16
LANES = 128
NT = (((1,), (1,)), ((), ()))
NN = (((1,), (0,)), ((), ()))


def nt(a, b):
    return lax.dot_general(a, b, NT, preferred_element_type=F32)


def nn(a, b):
    return lax.dot_general(a, b, NN, preferred_element_type=F32)


def cross_product(flow_velocity, vorticity):
    other = vorticity.astype(jnp.float32)
    first = flow_velocity[:, :, 1] * other[2] - flow_velocity[:, :, 2] * other[1]
    second = flow_velocity[:, :, 2] * other[0] - flow_velocity[:, :, 0] * other[2]
    third = flow_velocity[:, :, 0] * other[1] - flow_velocity[:, :, 1] * other[0]
    return jnp.stack([first, second, third]).astype(jnp.bfloat16)


def fourier_table(order_map, count):
    longitude = jnp.arange(count, dtype=jnp.int32)
    phase = order_map[:, None] * longitude[None, :] % count
    angle = phase.astype(jnp.float32) * (2.0 * math.pi / count)
    weight = jnp.where(order_map == 0, 1.0, 2.0).astype(jnp.float32)[:, None]
    return jnp.stack([weight * jnp.cos(angle), -weight * jnp.sin(angle)], axis=1).astype(
        jnp.bfloat16
    )


def plain_shards(spectral, inverse, legendre, vorticity, degree_list, order_map):
    orders = spectral.shape[3]
    shells = vorticity.shape[2]
    local_order_list = lax.dynamic_slice_in_dim(
        order_map, lax.axis_index("mem") * orders, orders
    )
    width = spectral.shape[0]
    flat = spectral.reshape(width, 6 * orders, spectral.shape[4])
    solved = lax.dot_general(
        inverse, flat, (((2,), (2,)), ((0,), (0,))), preferred_element_type=F32
    ).astype(BF16)
    moved = lax.all_to_all(solved, "grp", split_axis=1, concat_axis=0, tiled=True)
    by_order = jnp.transpose(
        moved.reshape(moved.shape[0], moved.shape[1] * 6, orders), (2, 0, 1)
    )
    segment = lax.all_gather(legendre, "grp", axis=2, tiled=True)
    allowed = local_order_list[:, None] <= degree_list[None, :]
    table = jnp.where(allowed[:, None, :], segment, jnp.zeros_like(segment))
    latitudinal = lax.dot_general(
        table, by_order, (((2,), (1,)), ((0,), (0,))), preferred_element_type=F32
    ).astype(BF16)
    gathered = lax.all_to_all(latitudinal, "mem", split_axis=1, concat_axis=0, tiled=True)
    arranged = gathered.reshape(gathered.shape[0], gathered.shape[1], shells, 3, 2)
    trig = fourier_table(order_map, vorticity.shape[3])
    velocity = jnp.einsum("mtsck,mkp->tscp", arranged, trig, preferred_element_type=F32)
    return cross_product(velocity, vorticity)


MESH = pl.DeviceIdType.MESH
CHUNKS = ((0, 1), (2,))
SLOTS = 6


def transfers(bufs, sems, send_ref, place):
    from_sib, to_far, from_far, to_mem, recv = bufs
    grp, me, core, sibling, across = place
    sib_s, sib_r, far_s, far_r, mem_s, mem_r = sems

    def to_sibling(j):
        return pltpu.make_async_remote_copy(
            src_ref=send_ref.at[j, 1 - core], dst_ref=from_sib.at[j],
            send_sem=sib_s.at[j], recv_sem=sib_r.at[j],
            device_id=(sibling, me), device_id_type=MESH,
        )

    def to_across(j):
        return pltpu.make_async_remote_copy(
            src_ref=to_far.at[j], dst_ref=from_far.at[j],
            send_sem=far_s.at[j], recv_sem=far_r.at[j],
            device_id=(across, me), device_id_type=MESH,
        )

    def to_member(j, slot):
        return pltpu.make_async_remote_copy(
            src_ref=to_mem.at[j], dst_ref=recv.at[slot],
            send_sem=mem_s.at[j], recv_sem=mem_r.at[slot],
            device_id=(grp, j), device_id_type=MESH,
        )

    return to_sibling, to_across, to_member


def synth_body(
    groups, members, spec_hbm, inv_hbm, leg_ref, deg_ref, ord_ref, *refs
):
    outs, refs = refs[: len(CHUNKS)], refs[len(CHUNKS) :]
    spec, inv, t0, t1, t2, main, rest, solved, f0, f1, f2, sems = refs[:12]
    refs = refs[12:]
    buffers = [refs[i * SLOTS : (i + 1) * SLOTS] for i in range(len(CHUNKS))]
    refs = refs[SLOTS * len(CHUNKS) :]
    sem_sets = [refs[i * 6 : (i + 1) * 6] for i in range(len(CHUNKS))]

    orders, radii, width = spec.shape[2:]
    shells = inv.shape[0]
    lats = leg_ref.shape[1]
    half = LANES // 2
    mine = shells // groups
    per_tile = LANES // orders
    pitch, lat_pitch = width + 1, orders + 1

    grp, me = lax.axis_index("grp"), lax.axis_index("mem")
    y, core = grp // 2, grp % 2
    sibling = y * 2 + (1 - core)
    across = (1 - y) * 2 + core
    place = (grp, me, core, sibling, across)

    barrier = pltpu.get_barrier_semaphore()
    for g in (sibling, across):
        pl.semaphore_signal(barrier, inc=1, device_id=(g, me), device_id_type=MESH)
    for i in range(1, members):
        pl.semaphore_signal(
            barrier, inc=1, device_id=(grp, (me + i) % members), device_id_type=MESH
        )

    inv_copy = pltpu.make_async_copy(inv_hbm, inv, sems.at[3])
    inv_copy.start()
    copies = [pltpu.make_async_copy(spec_hbm.at[c], spec.at[c], sems.at[c]) for c in range(3)]
    for copy in copies:
        copy.start()

    eye = (
        lax.broadcasted_iota(jnp.int32, (2 * width, 2 * width), 0)
        == lax.broadcasted_iota(jnp.int32, (2 * width, 2 * width), 1)
    ).astype(BF16)

    inv_copy.wait()

    def turn_inverse(i, carry):
        both = jnp.concatenate([inv[2 * i], inv[2 * i + 1]], axis=1)
        out = nt(eye, jnp.concatenate([both, both[LANES:]], axis=0))
        for h in range(2):
            at = pl.ds((2 * i + h) * pitch, width)
            part = out[h * width : (h + 1) * width]
            main[at, :] = part[:, 0:LANES]
            rest[at, :] = part[:, LANES : 2 * LANES]
        return carry

    lax.fori_loop(0, shells // 2, turn_inverse, 0, unroll=4)

    def turn(c):
        copies[c].wait()

        def turn_profiles(i, carry):
            a, b = [
                jnp.concatenate([spec[c, k, 2 * i], spec[c, k, 2 * i + 1]], axis=1)
                for k in range(2)
            ]
            out = nt(eye, jnp.concatenate([a, b[LANES:], b[:LANES]], axis=0))
            for h in range(2):
                at = pl.ds((c * orders + 2 * i + h) * pitch, width)
                part = out[h * width : (h + 1) * width]
                t0[at, :] = part[:, 0:LANES]
                t1[at, :] = part[:, LANES : 2 * LANES]
                t2[at, :] = part[:, 2 * LANES : 3 * LANES]
            return carry

        lax.fori_loop(0, orders // 2, turn_profiles, 0, unroll=4)

    nothing = jnp.zeros((shells, LANES), BF16)
    pad = jnp.zeros((half - shells, 3 * LANES), BF16)
    low = lax.broadcasted_iota(jnp.int32, (shells, LANES), 1) < half

    def solve_chunk(comps):
        def solve(l, carry):
            at = pl.ds(comps[0] * orders * pitch + l, len(comps) * orders, stride=pitch)
            profiles = jnp.concatenate([r[at, :].astype(BF16) for r in (t0, t1, t2)], axis=1)
            on = pl.ds(l, shells, stride=pitch)
            first, last = main[on, :].astype(BF16), rest[on, :]
            lower = jnp.where(low, last, 0.0).astype(BF16)
            upper = jnp.where(low, 0.0, last).astype(BF16)
            real = jnp.concatenate([first, lower, nothing], axis=1)
            imag = jnp.concatenate([nothing, upper, first], axis=1)
            solved[at, :] = nt(profiles, jnp.concatenate([real, pad, imag, pad], axis=0))
            return carry

        lax.fori_loop(0, width, solve, 0, unroll=16)

    degrees = deg_ref[pl.ds(pl.multiple_of(grp * width, width), width)].reshape(1, width)
    sums = (f0, f1, f2)

    def sum_chunk(comps):
        def sum_degrees(m, carry):
            valid = degrees >= ord_ref[me * orders + m]
            table = jnp.where(valid, leg_ref[m].astype(F32), 0.0).astype(BF16)
            block = jnp.concatenate(
                [
                    solved[pl.ds((c * orders + m) * pitch, width), :].astype(BF16)
                    for c in comps
                ],
                axis=1,
            )
            out = nn(table, block)
            at = pl.ds(m, lats, stride=lat_pitch)
            for i, c in enumerate(comps):
                sums[c][at, :] = out[:, i * LANES : (i + 1) * LANES]
            return carry

        lax.fori_loop(0, orders, sum_degrees, 0, unroll=8)

    row = lax.broadcasted_iota(jnp.int32, (2 * shells, LANES), 0)
    lane = lax.broadcasted_iota(jnp.int32, (2 * shells, LANES), 1)
    want = row
    for i in range(1, 2 * groups):
        g, k = i // 2, i % 2
        step = (half + g * mine - i * mine) if k else (g * mine - i * mine)
        want = jnp.where(row >= i * mine, row + step, want)
    pick = (want == lane).astype(BF16)
    tiles = lats // members // per_tile

    def target(i):
        return (me + 1 + i) % members

    def send_chunk(n):
        send_ref = buffers[n][0]
        to_sibling, _, _ = transfers(buffers[n][1:], sem_sets[n], send_ref, place)

        def turn_sums(i, carry):
            j = target(i)
            parts = []
            for b in range(tiles):
                at = [
                    pl.ds(((j * tiles + b) * per_tile + i) * lat_pitch, orders)
                    for i in range(per_tile)
                ]
                for c in CHUNKS[n]:
                    both = jnp.concatenate([sums[c][a, :].astype(BF16) for a in at], axis=0)
                    parts.append(nt(pick, both))
            for g in range(groups):
                block = [p[g * 2 * mine : (g + 1) * 2 * mine] for p in parts]
                send_ref[j, g % 2, g // 2] = jnp.concatenate(block, axis=0).astype(BF16)
            to_sibling(j).start()
            return carry

        lax.fori_loop(0, members, turn_sums, 0)

    def pair_sum(n, j, which):
        send_ref, from_sib = buffers[n][:2]
        return send_ref[j, core, which].astype(F32) + from_sib[j, which].astype(F32)

    def second(n):
        to_sibling, to_across, _ = transfers(buffers[n][1:], sem_sets[n], buffers[n][0], place)
        to_far = buffers[n][2]

        def step(i, carry):
            j = target(i)
            to_sibling(j).wait_recv()
            to_far[j] = pair_sum(n, j, 1 - y).astype(BF16)
            to_across(j).start()
            return carry

        lax.fori_loop(0, members, step, 0)

    def third(n):
        _, to_across, to_member = transfers(buffers[n][1:], sem_sets[n], buffers[n][0], place)
        _, _, _, from_far, to_mem, _ = buffers[n]

        def total(j):
            to_across(j).wait_recv()
            return (pair_sum(n, j, y) + from_far[j].astype(F32)).astype(BF16)

        def step(i, carry):
            j = target(i)
            to_mem[j] = total(j)
            to_member(j, me).start()
            return carry

        lax.fori_loop(0, members - 1, step, 0)
        outs[n][me] = total(me)

    def finish(n):
        moves = transfers(buffers[n][1:], sem_sets[n], buffers[n][0], place)
        to_sibling, to_across, to_member = moves
        recv = buffers[n][5]

        def step(i, carry):
            j = target(i)
            to_member(j, j).wait_recv()
            outs[n][j] = recv[j]
            to_member(j, me).wait_send()
            return carry

        lax.fori_loop(0, members - 1, step, 0)

        def drain(i, carry):
            to_sibling(i).wait_send()
            to_across(i).wait_send()
            return carry

        lax.fori_loop(0, members, drain, 0)

    last = len(CHUNKS) - 1
    for n, comps in enumerate(CHUNKS):
        for c in comps:
            turn(c)
        if n:
            second(n - 1)
        solve_chunk(comps)
        if n:
            third(n - 1)
        sum_chunk(comps)
        if n == 0:
            pl.semaphore_wait(barrier, members + 1)
        send_chunk(n)
    second(last)
    third(last)
    for n in range(len(CHUNKS)):
        finish(n)


def synthesize(spec, inv, legendre, degree_list, order_map, groups, members):
    _, _, orders, radii, width = spec.shape
    shells = inv.shape[0]
    lats = legendre.shape[1]
    mine = shells // groups
    pitch = width + 1
    any_space = pl.BlockSpec(memory_space=pl.ANY)
    vmem = pl.BlockSpec(memory_space=pltpu.VMEM)
    buffers, shapes = [], []
    for comps in CHUNKS:
        block = lats // members * orders * mine * 2 * len(comps) // LANES
        slots = pltpu.VMEM((members, block, LANES), BF16)
        buffers += [
            pltpu.VMEM((members, 2, groups // 2, block, LANES), BF16),
            pltpu.VMEM((members, groups // 2, block, LANES), BF16),
            slots, slots, slots, slots,
        ]
        shapes.append(jax.ShapeDtypeStruct((members, block, LANES), BF16))
    return pl.pallas_call(
        functools.partial(synth_body, groups, members),
        out_shape=shapes,
        in_specs=[any_space, any_space, vmem, vmem, pl.BlockSpec(memory_space=pltpu.SMEM)],
        out_specs=[vmem] * len(CHUNKS),
        scratch_shapes=[
            pltpu.VMEM(spec.shape, BF16),
            pltpu.VMEM(inv.shape, BF16),
            *[pltpu.VMEM((3 * orders * pitch, LANES), F32)] * 3,
            *[pltpu.VMEM((shells * pitch, LANES), F32)] * 2,
            pltpu.VMEM((3 * orders * pitch, LANES), F32),
            *[pltpu.VMEM((lats * (orders + 1), LANES), F32)] * 3,
            pltpu.SemaphoreType.DMA((4,)),
            *buffers,
            *[pltpu.SemaphoreType.DMA((members,))] * (6 * len(CHUNKS)),
        ],
        compiler_params=pltpu.CompilerParams(
            collective_id=0, has_side_effects=True, vmem_limit_bytes=60 * 2**20
        ),
        name="synthesize",
    )(spec, inv, legendre, degree_list, order_map)


def cos_sin(phase, count):
    phase = phase - count * jnp.floor((phase + 0.5) * (1.0 / count))
    turns = jnp.floor((phase + count / 8) * (4.0 / count))
    t = (phase - turns * (count / 4)) * (2.0 * math.pi / count)
    x = t * t
    s = t * (1 + x * (-1 / 6 + x * (1 / 120 + x * (-1 / 5040 + x * (1 / 362880)))))
    c = 1 + x * (
        -1 / 2 + x * (1 / 24 + x * (-1 / 720 + x * (1 / 40320 + x * (-1 / 3628800))))
    )
    odd = (turns == 1) | (turns == 3)
    cos, sin = jnp.where(odd, s, c), jnp.where(odd, c, s)
    cos = jnp.where((turns == 1) | (turns == 2), -cos, cos)
    sin = jnp.where((turns == 2) | (turns == 3), -sin, sin)
    return cos, sin


def physical_body(orders, *refs):
    recvs, refs = refs[: len(CHUNKS)], refs[len(CHUNKS) :]
    vort_hbm, ord_ref, out_ref, vort_ref, sem, *keep = refs
    copy = pltpu.make_async_copy(vort_hbm, vort_ref, sem.at[0])
    copy.start()
    members = recvs[0].shape[0]
    shells = vort_ref.shape[1]
    lats = vort_ref.shape[2]
    points = vort_ref.shape[3]
    every = members * orders
    per_tile = LANES // orders
    tiles = lats // per_tile
    for comps, recv_ref in zip(CHUNKS, recvs):
        for i in range(per_tile):
            for h in range(members // per_tile):
                parts = [
                    recv_ref[h * per_tile + j].astype(F32)[:, i * orders : (i + 1) * orders]
                    for j in range(per_tile)
                ]
                joined = jnp.concatenate(parts, axis=1)
                for b in range(tiles):
                    for n, c in enumerate(comps):
                        for k in range(2):
                            at = ((b * len(comps) + n) * 2 + k) * shells
                            to = pl.ds(
                                c * shells * lats + b * per_tile + i, shells, stride=lats
                            )
                            keep[k * (members // per_tile) + h][to, :] = joined[at : at + shells]
    left = jnp.concatenate([r[...].astype(BF16) for r in keep], axis=1)

    line = ord_ref[...].reshape(1, every).astype(F32)
    same = lax.broadcasted_iota(jnp.int32, (every, every), 0) == lax.broadcasted_iota(
        jnp.int32, (every, every), 1
    )
    column = jnp.sum(jnp.where(same, line, 0.0), axis=1, keepdims=True)
    lane = lax.broadcasted_iota(jnp.int32, (every, LANES), 1).astype(F32)
    nc, ns = cos_sin(column * lane, points)
    weight = jnp.where(column == 0.0, 1.0, 2.0)
    nc, ns = weight * nc, weight * ns
    far_c, far_s = cos_sin(column * (lane * LANES), points)

    flat = shells * lats
    copy.wait()
    for q in range(points // LANES):
        on = slice(q * LANES, (q + 1) * LANES)
        fc, fs = far_c[:, q : q + 1], far_s[:, q : q + 1]
        trig = jnp.concatenate([nc * fc - ns * fs, -(ns * fc + nc * fs)], axis=0).astype(BF16)
        v = nn(left, trig)
        v0, v1, v2 = v[:flat], v[flat : 2 * flat], v[2 * flat :]
        w0, w1, w2 = [vort_ref[c, :, :, on].reshape(flat, LANES).astype(F32) for c in range(3)]
        shape = (shells, lats, LANES)
        out_ref[0, :, :, on] = (v1 * w2 - v2 * w1).astype(BF16).reshape(shape)
        out_ref[1, :, :, on] = (v2 * w0 - v0 * w2).astype(BF16).reshape(shape)
        out_ref[2, :, :, on] = (v0 * w1 - v1 * w0).astype(BF16).reshape(shape)


def physical(received, vorticity, order_map, orders):
    members = received[0].shape[0]
    _, shells, lats, _ = vorticity.shape
    vmem = pl.BlockSpec(memory_space=pltpu.VMEM)
    return pl.pallas_call(
        functools.partial(physical_body, orders),
        out_shape=jax.ShapeDtypeStruct(vorticity.shape, BF16),
        in_specs=[vmem] * len(CHUNKS) + [pl.BlockSpec(memory_space=pl.ANY), vmem],
        out_specs=vmem,
        scratch_shapes=[pltpu.VMEM(vorticity.shape, BF16), pltpu.SemaphoreType.DMA((1,))]
        + [pltpu.VMEM((3 * shells * lats, LANES), F32)] * (2 * members * orders // LANES),
        compiler_params=pltpu.CompilerParams(vmem_limit_bytes=40 * 2**20),
        name="physical",
    )(*received, vorticity, order_map)


def shards(groups, members, spectral, inverse, legendre, vorticity, degree_list, order_map):
    orders = spectral.shape[3]
    spec = jnp.transpose(spectral, (1, 2, 3, 4, 0))
    inv = jnp.transpose(inverse, (1, 2, 0))
    vort = jnp.transpose(vorticity, (0, 2, 1, 3))
    received = synthesize(spec, inv, legendre, degree_list, order_map, groups, members)
    out = physical(received, vort, order_map, orders)
    return jnp.transpose(out, (0, 2, 1, 3))


def solution(mesh):
    groups, members = mesh.shape["grp"], mesh.shape["mem"]

    def local(spectral, inverse, legendre, vorticity, degree_list, order_map):
        args = (spectral, inverse, legendre, vorticity, degree_list, order_map)
        width, _, _, orders, radii = spectral.shape
        shells, lats = inverse.shape[1], legendre.shape[1]
        fits = (
            groups == 4
            and width == LANES
            and 2 * shells <= LANES
            and LANES < radii
            and 2 * radii == 3 * LANES
            and LANES % orders == 0
            and orders % 2 == 0
            and shells % 2 == 0
            and (shells // groups * 2) % 8 == 0
            and members % (LANES // orders) == 0
            and (lats // members) % (LANES // orders) == 0
            and vorticity.shape[3] % LANES == 0
            and vorticity.shape[3] // LANES <= LANES
            and members * orders * vorticity.shape[3] < 2**23
            and (lats // members) * orders * (shells // groups) * 2 % (16 * LANES) == 0
        )
        if fits:
            return shards(groups, members, *args)
        return plain_shards(*args)

    return jax.shard_map(
        local,
        mesh=mesh,
        in_specs=(
            P("grp", None, None, "mem", None),
            P("grp", None, None),
            P("mem", None, "grp"),
            P(None, "mem", "grp", None),
            P(),
            P(),
        ),
        out_specs=P(None, "mem", "grp", None),
        check_vma=False,
    )
```

```python
import functools
import math

import jax
import jax.numpy as jnp
from jax import lax
from jax.experimental import pallas as pl
from jax.experimental.pallas import tpu as pltpu
from jax.sharding import PartitionSpec as P

F32 = jnp.float32
BF16 = jnp.bfloat16
LANES = 128
NT = (((1,), (1,)), ((), ()))
NN = (((1,), (0,)), ((), ()))


def nt(a, b):
    return lax.dot_general(a, b, NT, preferred_element_type=F32)


def nn(a, b):
    return lax.dot_general(a, b, NN, preferred_element_type=F32)


def cross_product(flow_velocity, vorticity):
    other = vorticity.astype(jnp.float32)
    first = flow_velocity[:, :, 1] * other[2] - flow_velocity[:, :, 2] * other[1]
    second = flow_velocity[:, :, 2] * other[0] - flow_velocity[:, :, 0] * other[2]
    third = flow_velocity[:, :, 0] * other[1] - flow_velocity[:, :, 1] * other[0]
    return jnp.stack([first, second, third]).astype(jnp.bfloat16)


def fourier_table(order_map, count):
    longitude = jnp.arange(count, dtype=jnp.int32)
    phase = order_map[:, None] * longitude[None, :] % count
    angle = phase.astype(jnp.float32) * (2.0 * math.pi / count)
    weight = jnp.where(order_map == 0, 1.0, 2.0).astype(jnp.float32)[:, None]
    return jnp.stack([weight * jnp.cos(angle), -weight * jnp.sin(angle)], axis=1).astype(
        jnp.bfloat16
    )


def plain_shards(spectral, inverse, legendre, vorticity, degree_list, order_map):
    orders = spectral.shape[3]
    shells = vorticity.shape[2]
    local_order_list = lax.dynamic_slice_in_dim(
        order_map, lax.axis_index("mem") * orders, orders
    )
    width = spectral.shape[0]
    flat = spectral.reshape(width, 6 * orders, spectral.shape[4])
    solved = lax.dot_general(
        inverse, flat, (((2,), (2,)), ((0,), (0,))), preferred_element_type=F32
    ).astype(BF16)
    moved = lax.all_to_all(solved, "grp", split_axis=1, concat_axis=0, tiled=True)
    by_order = jnp.transpose(
        moved.reshape(moved.shape[0], moved.shape[1] * 6, orders), (2, 0, 1)
    )
    segment = lax.all_gather(legendre, "grp", axis=2, tiled=True)
    allowed = local_order_list[:, None] <= degree_list[None, :]
    table = jnp.where(allowed[:, None, :], segment, jnp.zeros_like(segment))
    latitudinal = lax.dot_general(
        table, by_order, (((2,), (1,)), ((0,), (0,))), preferred_element_type=F32
    ).astype(BF16)
    gathered = lax.all_to_all(latitudinal, "mem", split_axis=1, concat_axis=0, tiled=True)
    arranged = gathered.reshape(gathered.shape[0], gathered.shape[1], shells, 3, 2)
    trig = fourier_table(order_map, vorticity.shape[3])
    velocity = jnp.einsum("mtsck,mkp->tscp", arranged, trig, preferred_element_type=F32)
    return cross_product(velocity, vorticity)


MESH = pl.DeviceIdType.MESH
CHUNKS = ((0, 1), (2,))
SLOTS = 6


def transfers(bufs, sems, send_ref, place):
    from_sib, to_far, from_far, to_mem, recv = bufs
    grp, me, core, sibling, across = place
    sib_s, sib_r, far_s, far_r, mem_s, mem_r = sems

    def to_sibling(j):
        return pltpu.make_async_remote_copy(
            src_ref=send_ref.at[j, 1 - core], dst_ref=from_sib.at[j],
            send_sem=sib_s.at[j], recv_sem=sib_r.at[j],
            device_id=(sibling, me), device_id_type=MESH,
        )

    def to_across(j):
        return pltpu.make_async_remote_copy(
            src_ref=to_far.at[j], dst_ref=from_far.at[j],
            send_sem=far_s.at[j], recv_sem=far_r.at[j],
            device_id=(across, me), device_id_type=MESH,
        )

    def to_member(j, slot):
        return pltpu.make_async_remote_copy(
            src_ref=to_mem.at[j], dst_ref=recv.at[slot],
            send_sem=mem_s.at[j], recv_sem=mem_r.at[slot],
            device_id=(grp, j), device_id_type=MESH,
        )

    return to_sibling, to_across, to_member


def synth_body(
    groups, members, spec_hbm, inv_hbm, leg_hbm, deg_ref, ord_ref, *refs
):
    outs, refs = refs[: len(CHUNKS)], refs[len(CHUNKS) :]
    spec, inv, leg_ref, t0, t1, t2, main, rest, solved, f0, f1, f2, sems = refs[:13]
    refs = refs[13:]
    buffers = [refs[i * SLOTS : (i + 1) * SLOTS] for i in range(len(CHUNKS))]
    refs = refs[SLOTS * len(CHUNKS) :]
    sem_sets = [refs[i * 6 : (i + 1) * 6] for i in range(len(CHUNKS))]

    orders, radii, width = spec.shape[2:]
    shells = inv.shape[0]
    lats = leg_ref.shape[1]
    half = LANES // 2
    mine = shells // groups
    per_tile = LANES // orders
    pitch, lat_pitch = width + 1, orders + 1

    grp, me = lax.axis_index("grp"), lax.axis_index("mem")
    y, core = grp // 2, grp % 2
    sibling = y * 2 + (1 - core)
    across = (1 - y) * 2 + core
    place = (grp, me, core, sibling, across)

    barrier = pltpu.get_barrier_semaphore()
    for g in (sibling, across):
        pl.semaphore_signal(barrier, inc=1, device_id=(g, me), device_id_type=MESH)
    for i in range(1, members):
        pl.semaphore_signal(
            barrier, inc=1, device_id=(grp, (me + i) % members), device_id_type=MESH
        )

    inv_copy = pltpu.make_async_copy(inv_hbm, inv, sems.at[3])
    inv_copy.start()
    copies = [pltpu.make_async_copy(spec_hbm.at[c], spec.at[c], sems.at[c]) for c in range(3)]
    leg_copy = pltpu.make_async_copy(leg_hbm, leg_ref, sems.at[4])
    for copy in (*copies, leg_copy):
        copy.start()

    eye = (
        lax.broadcasted_iota(jnp.int32, (2 * width, 2 * width), 0)
        == lax.broadcasted_iota(jnp.int32, (2 * width, 2 * width), 1)
    ).astype(BF16)

    inv_copy.wait()

    def turn_inverse(i, carry):
        both = jnp.concatenate([inv[2 * i], inv[2 * i + 1]], axis=1)
        out = nt(eye, jnp.concatenate([both, both[LANES:]], axis=0))
        for h in range(2):
            at = pl.ds((2 * i + h) * pitch, width)
            part = out[h * width : (h + 1) * width]
            main[at, :] = part[:, 0:LANES]
            rest[at, :] = part[:, LANES : 2 * LANES]
        return carry

    lax.fori_loop(0, shells // 2, turn_inverse, 0, unroll=4)

    def turn(c):
        copies[c].wait()

        def turn_profiles(i, carry):
            a, b = [
                jnp.concatenate([spec[c, k, 2 * i], spec[c, k, 2 * i + 1]], axis=1)
                for k in range(2)
            ]
            out = nt(eye, jnp.concatenate([a, b[LANES:], b[:LANES]], axis=0))
            for h in range(2):
                at = pl.ds((c * orders + 2 * i + h) * pitch, width)
                part = out[h * width : (h + 1) * width]
                t0[at, :] = part[:, 0:LANES]
                t1[at, :] = part[:, LANES : 2 * LANES]
                t2[at, :] = part[:, 2 * LANES : 3 * LANES]
            return carry

        lax.fori_loop(0, orders // 2, turn_profiles, 0, unroll=4)

    pad = jnp.zeros((half - shells, 2 * LANES), BF16)

    def solve_chunk(comps):
        count = len(comps) * orders
        low = lax.broadcasted_iota(jnp.int32, (count, LANES), 1) < half

        def solve(l, carry):
            at = pl.ds(comps[0] * orders * pitch + l, count, stride=pitch)
            shared = t1[at, :]
            real = jnp.concatenate([t0[at, :], jnp.where(low, shared, 0.0)], axis=1)
            imag = jnp.concatenate([t2[at, :], jnp.where(low, 0.0, shared)], axis=1)
            profiles = jnp.concatenate([real, imag], axis=0).astype(BF16)
            on = pl.ds(l, shells, stride=pitch)
            weights = jnp.concatenate([main[on, :], rest[on, :]], axis=1).astype(BF16)
            out = nt(profiles, jnp.concatenate([weights, pad], axis=0))
            solved[at, :] = jnp.concatenate([out[:count], out[count:]], axis=1)
            return carry

        lax.fori_loop(0, width, solve, 0, unroll=16)

    degrees = deg_ref[pl.ds(pl.multiple_of(grp * width, width), width)].reshape(1, width)
    sums = (f0, f1, f2)

    def sum_chunk(comps):
        def sum_degrees(m, carry):
            valid = degrees >= ord_ref[me * orders + m]
            table = jnp.where(valid, leg_ref[m].astype(F32), 0.0).astype(BF16)
            block = jnp.concatenate(
                [
                    solved[pl.ds((c * orders + m) * pitch, width), :].astype(BF16)
                    for c in comps
                ],
                axis=1,
            )
            out = nn(table, block)
            at = pl.ds(m, lats, stride=lat_pitch)
            for i, c in enumerate(comps):
                sums[c][at, :] = out[:, i * LANES : (i + 1) * LANES]
            return carry

        lax.fori_loop(0, orders, sum_degrees, 0, unroll=8)

    row = lax.broadcasted_iota(jnp.int32, (2 * shells, LANES), 0)
    lane = lax.broadcasted_iota(jnp.int32, (2 * shells, LANES), 1)
    want = row
    for i in range(1, 2 * groups):
        g, k = i // 2, i % 2
        step = (half + g * mine - i * mine) if k else (g * mine - i * mine)
        want = jnp.where(row >= i * mine, row + step, want)
    pick = (want == lane).astype(BF16)
    tiles = lats // members // per_tile

    def target(i):
        return (me + 1 + i) % members

    def send_chunk(n):
        send_ref = buffers[n][0]
        to_sibling, _, _ = transfers(buffers[n][1:], sem_sets[n], send_ref, place)

        def turn_sums(i, carry):
            j = target(i)
            parts = []
            for b in range(tiles):
                at = [
                    pl.ds(((j * tiles + b) * per_tile + i) * lat_pitch, orders)
                    for i in range(per_tile)
                ]
                for c in CHUNKS[n]:
                    both = jnp.concatenate([sums[c][a, :].astype(BF16) for a in at], axis=0)
                    parts.append(nt(pick, both))
            for g in range(groups):
                block = [p[g * 2 * mine : (g + 1) * 2 * mine] for p in parts]
                send_ref[j, g % 2, g // 2] = jnp.concatenate(block, axis=0).astype(BF16)
            to_sibling(j).start()
            return carry

        lax.fori_loop(0, members, turn_sums, 0, unroll=2)

    def pair_sum(n, j, which):
        send_ref, from_sib = buffers[n][:2]
        return send_ref[j, core, which].astype(F32) + from_sib[j, which].astype(F32)

    def second(n):
        to_sibling, to_across, _ = transfers(buffers[n][1:], sem_sets[n], buffers[n][0], place)
        to_far = buffers[n][2]

        def step(i, carry):
            j = target(i)
            to_sibling(j).wait_recv()
            to_far[j] = pair_sum(n, j, 1 - y).astype(BF16)
            to_across(j).start()
            return carry

        lax.fori_loop(0, members, step, 0)

    def third(n):
        _, to_across, to_member = transfers(buffers[n][1:], sem_sets[n], buffers[n][0], place)
        _, _, _, from_far, to_mem, _ = buffers[n]

        def total(j):
            to_across(j).wait_recv()
            return (pair_sum(n, j, y) + from_far[j].astype(F32)).astype(BF16)

        def step(i, carry):
            j = target(i)
            to_mem[j] = total(j)
            to_member(j, me).start()
            return carry

        lax.fori_loop(0, members - 1, step, 0)
        outs[n][me] = total(me)

    def finish(n):
        moves = transfers(buffers[n][1:], sem_sets[n], buffers[n][0], place)
        to_sibling, to_across, to_member = moves
        recv = buffers[n][5]

        def step(i, carry):
            j = target(i)
            to_member(j, j).wait_recv()
            outs[n][j] = recv[j]
            to_member(j, me).wait_send()
            return carry

        lax.fori_loop(0, members - 1, step, 0)

        def drain(i, carry):
            to_sibling(i).wait_send()
            to_across(i).wait_send()
            return carry

        lax.fori_loop(0, members, drain, 0)

    last = len(CHUNKS) - 1
    for n, comps in enumerate(CHUNKS):
        for c in comps:
            turn(c)
        if n:
            second(n - 1)
        solve_chunk(comps)
        if n:
            third(n - 1)
        if n == 0:
            leg_copy.wait()
        sum_chunk(comps)
        if n == 0:
            pl.semaphore_wait(barrier, members + 1)
        send_chunk(n)
    second(last)
    third(last)
    for n in range(len(CHUNKS)):
        finish(n)


def synthesize(spec, inv, legendre, degree_list, order_map, groups, members):
    _, _, orders, radii, width = spec.shape
    shells = inv.shape[0]
    lats = legendre.shape[1]
    mine = shells // groups
    pitch = width + 1
    any_space = pl.BlockSpec(memory_space=pl.ANY)
    vmem = pl.BlockSpec(memory_space=pltpu.VMEM)
    buffers, shapes = [], []
    for comps in CHUNKS:
        block = lats // members * orders * mine * 2 * len(comps) // LANES
        slots = pltpu.VMEM((members, block, LANES), BF16)
        buffers += [
            pltpu.VMEM((members, 2, groups // 2, block, LANES), BF16),
            pltpu.VMEM((members, groups // 2, block, LANES), BF16),
            slots, slots, slots, slots,
        ]
        shapes.append(jax.ShapeDtypeStruct((members, block, LANES), BF16))
    return pl.pallas_call(
        functools.partial(synth_body, groups, members),
        out_shape=shapes,
        in_specs=[any_space] * 3 + [vmem, pl.BlockSpec(memory_space=pltpu.SMEM)],
        out_specs=[vmem] * len(CHUNKS),
        scratch_shapes=[
            pltpu.VMEM(spec.shape, BF16),
            pltpu.VMEM(inv.shape, BF16),
            pltpu.VMEM(legendre.shape, BF16),
            *[pltpu.VMEM((3 * orders * pitch, LANES), F32)] * 3,
            *[pltpu.VMEM((shells * pitch, LANES), F32)] * 2,
            pltpu.VMEM((3 * orders * pitch, LANES), F32),
            *[pltpu.VMEM((lats * (orders + 1), LANES), F32)] * 3,
            pltpu.SemaphoreType.DMA((5,)),
            *buffers,
            *[pltpu.SemaphoreType.DMA((members,))] * (6 * len(CHUNKS)),
        ],
        compiler_params=pltpu.CompilerParams(
            collective_id=0, has_side_effects=True, vmem_limit_bytes=52 * 2**20
        ),
        name="synthesize",
    )(spec, inv, legendre, degree_list, order_map)


def cos_sin(phase, count):
    phase = phase - count * jnp.floor((phase + 0.5) * (1.0 / count))
    turns = jnp.floor((phase + count / 8) * (4.0 / count))
    t = (phase - turns * (count / 4)) * (2.0 * math.pi / count)
    x = t * t
    s = t * (1 + x * (-1 / 6 + x * (1 / 120 + x * (-1 / 5040 + x * (1 / 362880)))))
    c = 1 + x * (
        -1 / 2 + x * (1 / 24 + x * (-1 / 720 + x * (1 / 40320 + x * (-1 / 3628800))))
    )
    odd = (turns == 1) | (turns == 3)
    cos, sin = jnp.where(odd, s, c), jnp.where(odd, c, s)
    cos = jnp.where((turns == 1) | (turns == 2), -cos, cos)
    sin = jnp.where((turns == 2) | (turns == 3), -sin, sin)
    return cos, sin


def physical_body(orders, *refs):
    recvs, refs = refs[: len(CHUNKS)], refs[len(CHUNKS) :]
    vort_hbm, ord_ref, out_ref, vort_ref, sem, *keep = refs
    held, keep = keep[: len(CHUNKS)], keep[len(CHUNKS) :]
    copy = pltpu.make_async_copy(vort_hbm, vort_ref, sem.at[0])
    arrivals = [
        pltpu.make_async_copy(r, h, sem.at[1 + n]) for n, (r, h) in enumerate(zip(recvs, held))
    ]
    for arrival in arrivals:
        arrival.start()
    copy.start()
    members = recvs[0].shape[0]
    shells = vort_ref.shape[1]
    lats = vort_ref.shape[2]
    points = vort_ref.shape[3]
    every = members * orders
    per_tile = LANES // orders
    tiles = lats // per_tile
    line = ord_ref[...].reshape(1, every).astype(F32)
    same = lax.broadcasted_iota(jnp.int32, (every, every), 0) == lax.broadcasted_iota(
        jnp.int32, (every, every), 1
    )
    column = jnp.sum(jnp.where(same, line, 0.0), axis=1, keepdims=True)
    lane = lax.broadcasted_iota(jnp.int32, (every, LANES), 1).astype(F32)
    nc, ns = cos_sin(column * lane, points)
    weight = jnp.where(column == 0.0, 1.0, 2.0)
    nc, ns = weight * nc, weight * ns
    far_c, far_s = cos_sin(column * (lane * LANES), points)

    for arrival in arrivals:
        arrival.wait()
    for comps, recv_ref in zip(CHUNKS, held):
        for i in range(per_tile):
            for h in range(members // per_tile):
                parts = [
                    recv_ref[h * per_tile + j].astype(F32)[:, i * orders : (i + 1) * orders]
                    for j in range(per_tile)
                ]
                joined = jnp.concatenate(parts, axis=1)
                for b in range(tiles):
                    for n, c in enumerate(comps):
                        for k in range(2):
                            at = ((b * len(comps) + n) * 2 + k) * shells
                            to = pl.ds(
                                c * shells * lats + b * per_tile + i, shells, stride=lats
                            )
                            keep[k * (members // per_tile) + h][to, :] = joined[at : at + shells]
    left = jnp.concatenate([r[...].astype(BF16) for r in keep], axis=1)

    flat = shells * lats
    copy.wait()
    for q in range(points // LANES):
        on = slice(q * LANES, (q + 1) * LANES)
        fc, fs = far_c[:, q : q + 1], far_s[:, q : q + 1]
        trig = jnp.concatenate([nc * fc - ns * fs, -(ns * fc + nc * fs)], axis=0).astype(BF16)
        v = nn(left, trig)
        v0, v1, v2 = v[:flat], v[flat : 2 * flat], v[2 * flat :]
        w0, w1, w2 = [vort_ref[c, :, :, on].reshape(flat, LANES).astype(F32) for c in range(3)]
        shape = (shells, lats, LANES)
        out_ref[0, :, :, on] = (v1 * w2 - v2 * w1).astype(BF16).reshape(shape)
        out_ref[1, :, :, on] = (v2 * w0 - v0 * w2).astype(BF16).reshape(shape)
        out_ref[2, :, :, on] = (v0 * w1 - v1 * w0).astype(BF16).reshape(shape)


def physical(received, vorticity, order_map, orders):
    members = received[0].shape[0]
    _, shells, lats, _ = vorticity.shape
    vmem = pl.BlockSpec(memory_space=pltpu.VMEM)
    return pl.pallas_call(
        functools.partial(physical_body, orders),
        out_shape=jax.ShapeDtypeStruct(vorticity.shape, BF16),
        in_specs=[pl.BlockSpec(memory_space=pl.ANY)] * (len(CHUNKS) + 1) + [vmem],
        out_specs=vmem,
        scratch_shapes=[
            pltpu.VMEM(vorticity.shape, BF16),
            pltpu.SemaphoreType.DMA((1 + len(CHUNKS),)),
        ]
        + [pltpu.VMEM(r.shape, BF16) for r in received]
        + [pltpu.VMEM((3 * shells * lats, LANES), F32)] * (2 * members * orders // LANES),
        compiler_params=pltpu.CompilerParams(vmem_limit_bytes=24 * 2**20),
        name="physical",
    )(*received, vorticity, order_map)


def shards(groups, members, spectral, inverse, legendre, vorticity, degree_list, order_map):
    orders = spectral.shape[3]
    spec = jnp.transpose(spectral, (1, 2, 3, 4, 0))
    inv = jnp.transpose(inverse, (1, 2, 0))
    vort = jnp.transpose(vorticity, (0, 2, 1, 3))
    received = synthesize(spec, inv, legendre, degree_list, order_map, groups, members)
    out = physical(received, vort, order_map, orders)
    return jnp.transpose(out, (0, 2, 1, 3))


def solution(mesh):
    groups, members = mesh.shape["grp"], mesh.shape["mem"]

    def local(spectral, inverse, legendre, vorticity, degree_list, order_map):
        args = (spectral, inverse, legendre, vorticity, degree_list, order_map)
        width, _, _, orders, radii = spectral.shape
        shells, lats = inverse.shape[1], legendre.shape[1]
        fits = (
            groups == 4
            and width == LANES
            and 2 * shells <= LANES
            and LANES < radii
            and 2 * radii == 3 * LANES
            and LANES % orders == 0
            and orders % 2 == 0
            and shells % 2 == 0
            and (shells // groups * 2) % 8 == 0
            and members % (LANES // orders) == 0
            and (lats // members) % (LANES // orders) == 0
            and vorticity.shape[3] % LANES == 0
            and vorticity.shape[3] // LANES <= LANES
            and members * orders * vorticity.shape[3] < 2**23
            and (lats // members) * orders * (shells // groups) * 2 % (16 * LANES) == 0
        )
        if fits:
            return shards(groups, members, *args)
        return plain_shards(*args)

    return jax.shard_map(
        local,
        mesh=mesh,
        in_specs=(
            P("grp", None, None, "mem", None),
            P("grp", None, None),
            P("mem", None, "grp"),
            P(None, "mem", "grp", None),
            P(),
            P(),
        ),
        out_specs=P(None, "mem", "grp", None),
        check_vma=False,
    )
```

```python
import functools
import math

import jax
import jax.numpy as jnp
from jax import lax
from jax.experimental import pallas as pl
from jax.experimental.pallas import tpu as pltpu
from jax.sharding import PartitionSpec as P

F32 = jnp.float32
BF16 = jnp.bfloat16
LANES = 128
NT = (((1,), (1,)), ((), ()))
NN = (((1,), (0,)), ((), ()))


def nt(a, b):
    return lax.dot_general(a, b, NT, preferred_element_type=F32)


def nn(a, b):
    return lax.dot_general(a, b, NN, preferred_element_type=F32)


def cross_product(flow_velocity, vorticity):
    other = vorticity.astype(jnp.float32)
    first = flow_velocity[:, :, 1] * other[2] - flow_velocity[:, :, 2] * other[1]
    second = flow_velocity[:, :, 2] * other[0] - flow_velocity[:, :, 0] * other[2]
    third = flow_velocity[:, :, 0] * other[1] - flow_velocity[:, :, 1] * other[0]
    return jnp.stack([first, second, third]).astype(jnp.bfloat16)


def fourier_table(order_map, count):
    longitude = jnp.arange(count, dtype=jnp.int32)
    phase = order_map[:, None] * longitude[None, :] % count
    angle = phase.astype(jnp.float32) * (2.0 * math.pi / count)
    weight = jnp.where(order_map == 0, 1.0, 2.0).astype(jnp.float32)[:, None]
    return jnp.stack([weight * jnp.cos(angle), -weight * jnp.sin(angle)], axis=1).astype(
        jnp.bfloat16
    )


def plain_shards(spectral, inverse, legendre, vorticity, degree_list, order_map):
    orders = spectral.shape[3]
    shells = vorticity.shape[2]
    local_order_list = lax.dynamic_slice_in_dim(
        order_map, lax.axis_index("mem") * orders, orders
    )
    width = spectral.shape[0]
    flat = spectral.reshape(width, 6 * orders, spectral.shape[4])
    solved = lax.dot_general(
        inverse, flat, (((2,), (2,)), ((0,), (0,))), preferred_element_type=F32
    ).astype(BF16)
    moved = lax.all_to_all(solved, "grp", split_axis=1, concat_axis=0, tiled=True)
    by_order = jnp.transpose(
        moved.reshape(moved.shape[0], moved.shape[1] * 6, orders), (2, 0, 1)
    )
    segment = lax.all_gather(legendre, "grp", axis=2, tiled=True)
    allowed = local_order_list[:, None] <= degree_list[None, :]
    table = jnp.where(allowed[:, None, :], segment, jnp.zeros_like(segment))
    latitudinal = lax.dot_general(
        table, by_order, (((2,), (1,)), ((0,), (0,))), preferred_element_type=F32
    ).astype(BF16)
    gathered = lax.all_to_all(latitudinal, "mem", split_axis=1, concat_axis=0, tiled=True)
    arranged = gathered.reshape(gathered.shape[0], gathered.shape[1], shells, 3, 2)
    trig = fourier_table(order_map, vorticity.shape[3])
    velocity = jnp.einsum("mtsck,mkp->tscp", arranged, trig, preferred_element_type=F32)
    return cross_product(velocity, vorticity)


MESH = pl.DeviceIdType.MESH
CHUNKS = ((0, 1), (2,))
SLOTS = 6


def transfers(bufs, sems, send_ref, place):
    from_sib, to_far, from_far, to_mem, recv = bufs
    grp, me, core, sibling, across = place
    sib_s, sib_r, far_s, far_r, mem_s, mem_r = sems

    def to_sibling(j):
        return pltpu.make_async_remote_copy(
            src_ref=send_ref.at[j, 1 - core], dst_ref=from_sib.at[j],
            send_sem=sib_s.at[j], recv_sem=sib_r.at[j],
            device_id=(sibling, me), device_id_type=MESH,
        )

    def to_across(j):
        return pltpu.make_async_remote_copy(
            src_ref=to_far.at[j], dst_ref=from_far.at[j],
            send_sem=far_s.at[j], recv_sem=far_r.at[j],
            device_id=(across, me), device_id_type=MESH,
        )

    def to_member(j, slot):
        return pltpu.make_async_remote_copy(
            src_ref=to_mem.at[j], dst_ref=recv.at[slot],
            send_sem=mem_s.at[j], recv_sem=mem_r.at[slot],
            device_id=(grp, j), device_id_type=MESH,
        )

    return to_sibling, to_across, to_member


def synth_body(
    groups, members, spec_hbm, inv_hbm, leg_hbm, deg_ref, ord_ref, *refs
):
    outs, refs = refs[: len(CHUNKS)], refs[len(CHUNKS) :]
    spec, inv, leg_ref, t0, t1, t2, main, rest, solved, f0, f1, f2, sems = refs[:13]
    refs = refs[13:]
    buffers = [refs[i * SLOTS : (i + 1) * SLOTS] for i in range(len(CHUNKS))]
    refs = refs[SLOTS * len(CHUNKS) :]
    sem_sets = [refs[i * 6 : (i + 1) * 6] for i in range(len(CHUNKS))]

    orders, radii, width = spec.shape[2:]
    shells = inv.shape[0]
    lats = leg_ref.shape[1]
    half = LANES // 2
    mine = shells // groups
    per_tile = LANES // orders
    pitch, lat_pitch = width + 1, orders + 1

    grp, me = lax.axis_index("grp"), lax.axis_index("mem")
    y, core = grp // 2, grp % 2
    sibling = y * 2 + (1 - core)
    across = (1 - y) * 2 + core
    place = (grp, me, core, sibling, across)

    barrier = pltpu.get_barrier_semaphore()
    for g in (sibling, across):
        pl.semaphore_signal(barrier, inc=1, device_id=(g, me), device_id_type=MESH)
    for i in range(1, members):
        pl.semaphore_signal(
            barrier, inc=1, device_id=(grp, (me + i) % members), device_id_type=MESH
        )

    inv_copy = pltpu.make_async_copy(inv_hbm, inv, sems.at[3])
    inv_copy.start()
    copies = [pltpu.make_async_copy(spec_hbm.at[c], spec.at[c], sems.at[c]) for c in range(3)]
    leg_copy = pltpu.make_async_copy(leg_hbm, leg_ref, sems.at[4])
    for copy in (*copies, leg_copy):
        copy.start()

    eye = (
        lax.broadcasted_iota(jnp.int32, (2 * width, 2 * width), 0)
        == lax.broadcasted_iota(jnp.int32, (2 * width, 2 * width), 1)
    ).astype(BF16)

    inv_copy.wait()

    def turn_inverse(i, carry):
        both = jnp.concatenate([inv[2 * i], inv[2 * i + 1]], axis=1)
        out = nt(eye, jnp.concatenate([both, both[LANES:]], axis=0))
        for h in range(2):
            at = pl.ds((2 * i + h) * pitch, width)
            part = out[h * width : (h + 1) * width]
            main[at, :] = part[:, 0:LANES]
            rest[at, :] = part[:, LANES : 2 * LANES]
        return carry

    lax.fori_loop(0, shells // 2, turn_inverse, 0, unroll=8)

    def turn(c):
        copies[c].wait()

        def turn_profiles(i, carry):
            a, b = [
                jnp.concatenate([spec[c, k, 2 * i], spec[c, k, 2 * i + 1]], axis=1)
                for k in range(2)
            ]
            out = nt(eye, jnp.concatenate([a, b[LANES:], b[:LANES]], axis=0))
            for h in range(2):
                at = pl.ds((c * orders + 2 * i + h) * pitch, width)
                part = out[h * width : (h + 1) * width]
                t0[at, :] = part[:, 0:LANES]
                t1[at, :] = part[:, LANES : 2 * LANES]
                t2[at, :] = part[:, 2 * LANES : 3 * LANES]
            return carry

        lax.fori_loop(0, orders // 2, turn_profiles, 0, unroll=8)

    pad = jnp.zeros((half - shells, 2 * LANES), BF16)

    def solve_chunk(comps):
        count = len(comps) * orders
        low = lax.broadcasted_iota(jnp.int32, (count, LANES), 1) < half

        def solve(l, carry):
            at = pl.ds(comps[0] * orders * pitch + l, count, stride=pitch)
            shared = t1[at, :]
            real = jnp.concatenate([t0[at, :], jnp.where(low, shared, 0.0)], axis=1)
            imag = jnp.concatenate([t2[at, :], jnp.where(low, 0.0, shared)], axis=1)
            profiles = jnp.concatenate([real, imag], axis=0).astype(BF16)
            on = pl.ds(l, shells, stride=pitch)
            weights = jnp.concatenate([main[on, :], rest[on, :]], axis=1).astype(BF16)
            out = nt(profiles, jnp.concatenate([weights, pad], axis=0))
            solved[at, :] = jnp.concatenate([out[:count], out[count:]], axis=1)
            return carry

        lax.fori_loop(0, width, solve, 0, unroll=16)

    degrees = deg_ref[pl.ds(pl.multiple_of(grp * width, width), width)].reshape(1, width)
    sums = (f0, f1, f2)

    def sum_chunk(comps):
        def sum_degrees(m, carry):
            valid = degrees >= ord_ref[me * orders + m]
            table = jnp.where(valid, leg_ref[m].astype(F32), 0.0).astype(BF16)
            block = jnp.concatenate(
                [
                    solved[pl.ds((c * orders + m) * pitch, width), :].astype(BF16)
                    for c in comps
                ],
                axis=1,
            )
            out = nn(table, block)
            at = pl.ds(m, lats, stride=lat_pitch)
            for i, c in enumerate(comps):
                sums[c][at, :] = out[:, i * LANES : (i + 1) * LANES]
            return carry

        lax.fori_loop(0, orders, sum_degrees, 0, unroll=8)

    row = lax.broadcasted_iota(jnp.int32, (2 * shells, LANES), 0)
    lane = lax.broadcasted_iota(jnp.int32, (2 * shells, LANES), 1)
    want = row
    for i in range(1, 2 * groups):
        g, k = i // 2, i % 2
        step = (half + g * mine - i * mine) if k else (g * mine - i * mine)
        want = jnp.where(row >= i * mine, row + step, want)
    pick = (want == lane).astype(BF16)
    tiles = lats // members // per_tile

    def target(i):
        return (me + 1 + i) % members

    def pair_sum(n, j, which):
        send_ref, from_sib = buffers[n][:2]
        return send_ref[j, core, which].astype(F32) + from_sib[j, which].astype(F32)

    def send_chunk(n):
        send_ref, _, to_far = buffers[n][:3]
        to_sibling, to_across, _ = transfers(buffers[n][1:], sem_sets[n], send_ref, place)
        lag = 2

        def first(i):
            j = target(i)
            parts = []
            for b in range(tiles):
                at = [
                    pl.ds(((j * tiles + b) * per_tile + i) * lat_pitch, orders)
                    for i in range(per_tile)
                ]
                for c in CHUNKS[n]:
                    both = jnp.concatenate([sums[c][a, :].astype(BF16) for a in at], axis=0)
                    parts.append(nt(pick, both))
            for g in range(groups):
                block = [p[g * 2 * mine : (g + 1) * 2 * mine] for p in parts]
                send_ref[j, g % 2, g // 2] = jnp.concatenate(block, axis=0).astype(BF16)
            to_sibling(j).start()

        def second(i):
            j = target(i)
            to_sibling(j).wait_recv()
            to_far[j] = pair_sum(n, j, 1 - y).astype(BF16)
            to_across(j).start()

        def step(i, carry):
            first(i + lag)
            second(i)
            return carry

        for i in range(lag):
            first(i)
        lax.fori_loop(0, members - lag, step, 0)
        for i in range(members - lag, members):
            second(i)

    def third(n):
        _, to_across, to_member = transfers(buffers[n][1:], sem_sets[n], buffers[n][0], place)
        _, _, _, from_far, to_mem, _ = buffers[n]

        def total(j):
            to_across(j).wait_recv()
            return (pair_sum(n, j, y) + from_far[j].astype(F32)).astype(BF16)

        def step(i, carry):
            j = target(i)
            to_mem[j] = total(j)
            to_member(j, me).start()
            return carry

        lax.fori_loop(0, members - 1, step, 0)
        outs[n][me] = total(me)

    def finish(n):
        moves = transfers(buffers[n][1:], sem_sets[n], buffers[n][0], place)
        to_sibling, to_across, to_member = moves
        recv = buffers[n][5]

        def step(i, carry):
            j = target(i)
            to_member(j, j).wait_recv()
            outs[n][j] = recv[j]
            to_member(j, me).wait_send()
            return carry

        lax.fori_loop(0, members - 1, step, 0)

        def drain(i, carry):
            to_sibling(i).wait_send()
            to_across(i).wait_send()
            return carry

        lax.fori_loop(0, members, drain, 0)

    last = len(CHUNKS) - 1
    for n, comps in enumerate(CHUNKS):
        for c in comps:
            turn(c)
        solve_chunk(comps)
        if n:
            third(n - 1)
        if n == 0:
            leg_copy.wait()
        sum_chunk(comps)
        if n == 0:
            pl.semaphore_wait(barrier, members + 1)
        send_chunk(n)
    third(last)
    for n in range(len(CHUNKS)):
        finish(n)


def synthesize(spec, inv, legendre, degree_list, order_map, groups, members):
    _, _, orders, radii, width = spec.shape
    shells = inv.shape[0]
    lats = legendre.shape[1]
    mine = shells // groups
    pitch = width + 1
    any_space = pl.BlockSpec(memory_space=pl.ANY)
    vmem = pl.BlockSpec(memory_space=pltpu.VMEM)
    buffers, shapes = [], []
    for comps in CHUNKS:
        block = lats // members * orders * mine * 2 * len(comps) // LANES
        slots = pltpu.VMEM((members, block, LANES), BF16)
        buffers += [
            pltpu.VMEM((members, 2, groups // 2, block, LANES), BF16),
            pltpu.VMEM((members, groups // 2, block, LANES), BF16),
            slots, slots, slots, slots,
        ]
        shapes.append(jax.ShapeDtypeStruct((members, block, LANES), BF16))
    return pl.pallas_call(
        functools.partial(synth_body, groups, members),
        out_shape=shapes,
        in_specs=[any_space] * 3 + [vmem, pl.BlockSpec(memory_space=pltpu.SMEM)],
        out_specs=[vmem] * len(CHUNKS),
        scratch_shapes=[
            pltpu.VMEM(spec.shape, BF16),
            pltpu.VMEM(inv.shape, BF16),
            pltpu.VMEM(legendre.shape, BF16),
            *[pltpu.VMEM((3 * orders * pitch, LANES), F32)] * 3,
            *[pltpu.VMEM((shells * pitch, LANES), F32)] * 2,
            pltpu.VMEM((3 * orders * pitch, LANES), F32),
            *[pltpu.VMEM((lats * (orders + 1), LANES), F32)] * 3,
            pltpu.SemaphoreType.DMA((5,)),
            *buffers,
            *[pltpu.SemaphoreType.DMA((members,))] * (6 * len(CHUNKS)),
        ],
        compiler_params=pltpu.CompilerParams(
            collective_id=0, has_side_effects=True, vmem_limit_bytes=60 * 2**20
        ),
        name="synthesize",
    )(spec, inv, legendre, degree_list, order_map)


def cos_sin(phase, count):
    phase = phase - count * jnp.floor((phase + 0.5) * (1.0 / count))
    turns = jnp.floor((phase + count / 8) * (4.0 / count))
    t = (phase - turns * (count / 4)) * (2.0 * math.pi / count)
    x = t * t
    s = t * (1 + x * (-1 / 6 + x * (1 / 120 + x * (-1 / 5040 + x * (1 / 362880)))))
    c = 1 + x * (
        -1 / 2 + x * (1 / 24 + x * (-1 / 720 + x * (1 / 40320 + x * (-1 / 3628800))))
    )
    odd = (turns == 1) | (turns == 3)
    cos, sin = jnp.where(odd, s, c), jnp.where(odd, c, s)
    cos = jnp.where((turns == 1) | (turns == 2), -cos, cos)
    sin = jnp.where((turns == 2) | (turns == 3), -sin, sin)
    return cos, sin


def physical_body(orders, *refs):
    recvs, refs = refs[: len(CHUNKS)], refs[len(CHUNKS) :]
    vort_hbm, ord_ref, out_ref, vort_ref, sem, *keep = refs
    held, keep = keep[: len(CHUNKS)], keep[len(CHUNKS) :]
    copy = pltpu.make_async_copy(vort_hbm, vort_ref, sem.at[0])
    arrivals = [
        pltpu.make_async_copy(r, h, sem.at[1 + n]) for n, (r, h) in enumerate(zip(recvs, held))
    ]
    for arrival in arrivals:
        arrival.start()
    copy.start()
    members = recvs[0].shape[0]
    shells = vort_ref.shape[1]
    lats = vort_ref.shape[2]
    points = vort_ref.shape[3]
    every = members * orders
    per_tile = LANES // orders
    tiles = lats // per_tile
    line = ord_ref[...].reshape(1, every).astype(F32)
    same = lax.broadcasted_iota(jnp.int32, (every, every), 0) == lax.broadcasted_iota(
        jnp.int32, (every, every), 1
    )
    column = jnp.sum(jnp.where(same, line, 0.0), axis=1, keepdims=True)
    lane = lax.broadcasted_iota(jnp.int32, (every, LANES), 1).astype(F32)
    nc, ns = cos_sin(column * lane, points)
    weight = jnp.where(column == 0.0, 1.0, 2.0)
    nc, ns = weight * nc, weight * ns
    far_c, far_s = cos_sin(column * (lane * LANES), points)

    for arrival in arrivals:
        arrival.wait()
    for comps, recv_ref in zip(CHUNKS, held):
        for i in range(per_tile):
            for h in range(members // per_tile):
                parts = [
                    recv_ref[h * per_tile + j].astype(F32)[:, i * orders : (i + 1) * orders]
                    for j in range(per_tile)
                ]
                joined = jnp.concatenate(parts, axis=1)
                for b in range(tiles):
                    for n, c in enumerate(comps):
                        for k in range(2):
                            at = ((b * len(comps) + n) * 2 + k) * shells
                            to = pl.ds(
                                c * shells * lats + b * per_tile + i, shells, stride=lats
                            )
                            keep[k * (members // per_tile) + h][to, :] = joined[at : at + shells]
    left = jnp.concatenate([r[...].astype(BF16) for r in keep], axis=1)

    flat = shells * lats
    copy.wait()
    for q in range(points // LANES):
        on = slice(q * LANES, (q + 1) * LANES)
        fc, fs = far_c[:, q : q + 1], far_s[:, q : q + 1]
        trig = jnp.concatenate([nc * fc - ns * fs, -(ns * fc + nc * fs)], axis=0).astype(BF16)
        v = nn(left, trig)
        v0, v1, v2 = v[:flat], v[flat : 2 * flat], v[2 * flat :]
        w0, w1, w2 = [vort_ref[c, :, :, on].reshape(flat, LANES).astype(F32) for c in range(3)]
        shape = (shells, lats, LANES)
        out_ref[0, :, :, on] = (v1 * w2 - v2 * w1).astype(BF16).reshape(shape)
        out_ref[1, :, :, on] = (v2 * w0 - v0 * w2).astype(BF16).reshape(shape)
        out_ref[2, :, :, on] = (v0 * w1 - v1 * w0).astype(BF16).reshape(shape)


def physical(received, vorticity, order_map, orders):
    members = received[0].shape[0]
    _, shells, lats, _ = vorticity.shape
    vmem = pl.BlockSpec(memory_space=pltpu.VMEM)
    return pl.pallas_call(
        functools.partial(physical_body, orders),
        out_shape=jax.ShapeDtypeStruct(vorticity.shape, BF16),
        in_specs=[pl.BlockSpec(memory_space=pl.ANY)] * (len(CHUNKS) + 1) + [vmem],
        out_specs=vmem,
        scratch_shapes=[
            pltpu.VMEM(vorticity.shape, BF16),
            pltpu.SemaphoreType.DMA((1 + len(CHUNKS),)),
        ]
        + [pltpu.VMEM(r.shape, BF16) for r in received]
        + [pltpu.VMEM((3 * shells * lats, LANES), F32)] * (2 * members * orders // LANES),
        compiler_params=pltpu.CompilerParams(vmem_limit_bytes=24 * 2**20),
        name="physical",
    )(*received, vorticity, order_map)


def shards(groups, members, spectral, inverse, legendre, vorticity, degree_list, order_map):
    orders = spectral.shape[3]
    spec = jnp.transpose(spectral, (1, 2, 3, 4, 0))
    inv = jnp.transpose(inverse, (1, 2, 0))
    vort = jnp.transpose(vorticity, (0, 2, 1, 3))
    received = synthesize(spec, inv, legendre, degree_list, order_map, groups, members)
    out = physical(received, vort, order_map, orders)
    return jnp.transpose(out, (0, 2, 1, 3))


def solution(mesh):
    groups, members = mesh.shape["grp"], mesh.shape["mem"]

    def local(spectral, inverse, legendre, vorticity, degree_list, order_map):
        args = (spectral, inverse, legendre, vorticity, degree_list, order_map)
        width, _, _, orders, radii = spectral.shape
        shells, lats = inverse.shape[1], legendre.shape[1]
        fits = (
            groups == 4
            and width == LANES
            and 2 * shells <= LANES
            and LANES < radii
            and 2 * radii == 3 * LANES
            and LANES % orders == 0
            and orders % 2 == 0
            and shells % 2 == 0
            and (shells // groups * 2) % 8 == 0
            and members % (LANES // orders) == 0
            and (lats // members) % (LANES // orders) == 0
            and vorticity.shape[3] % LANES == 0
            and vorticity.shape[3] // LANES <= LANES
            and members * orders * vorticity.shape[3] < 2**23
            and (lats // members) * orders * (shells // groups) * 2 % (16 * LANES) == 0
        )
        if fits:
            return shards(groups, members, *args)
        return plain_shards(*args)

    return jax.shard_map(
        local,
        mesh=mesh,
        in_specs=(
            P("grp", None, None, "mem", None),
            P("grp", None, None),
            P("mem", None, "grp"),
            P(None, "mem", "grp", None),
            P(),
            P(),
        ),
        out_specs=P(None, "mem", "grp", None),
        check_vma=False,
    )
```

```python
import functools
import math

import jax
import jax.numpy as jnp
from jax import lax
from jax.experimental import pallas as pl
from jax.experimental.pallas import tpu as pltpu
from jax.sharding import PartitionSpec as P

F32 = jnp.float32
BF16 = jnp.bfloat16
LANES = 128
NT = (((1,), (1,)), ((), ()))
NN = (((1,), (0,)), ((), ()))


def nt(a, b):
    return lax.dot_general(a, b, NT, preferred_element_type=F32)


def nn(a, b):
    return lax.dot_general(a, b, NN, preferred_element_type=F32)


def cross_product(flow_velocity, vorticity):
    other = vorticity.astype(jnp.float32)
    first = flow_velocity[:, :, 1] * other[2] - flow_velocity[:, :, 2] * other[1]
    second = flow_velocity[:, :, 2] * other[0] - flow_velocity[:, :, 0] * other[2]
    third = flow_velocity[:, :, 0] * other[1] - flow_velocity[:, :, 1] * other[0]
    return jnp.stack([first, second, third]).astype(jnp.bfloat16)


def fourier_table(order_map, count):
    longitude = jnp.arange(count, dtype=jnp.int32)
    phase = order_map[:, None] * longitude[None, :] % count
    angle = phase.astype(jnp.float32) * (2.0 * math.pi / count)
    weight = jnp.where(order_map == 0, 1.0, 2.0).astype(jnp.float32)[:, None]
    return jnp.stack([weight * jnp.cos(angle), -weight * jnp.sin(angle)], axis=1).astype(
        jnp.bfloat16
    )


def plain_shards(spectral, inverse, legendre, vorticity, degree_list, order_map):
    orders = spectral.shape[3]
    shells = vorticity.shape[2]
    local_order_list = lax.dynamic_slice_in_dim(
        order_map, lax.axis_index("mem") * orders, orders
    )
    width = spectral.shape[0]
    flat = spectral.reshape(width, 6 * orders, spectral.shape[4])
    solved = lax.dot_general(
        inverse, flat, (((2,), (2,)), ((0,), (0,))), preferred_element_type=F32
    ).astype(BF16)
    moved = lax.all_to_all(solved, "grp", split_axis=1, concat_axis=0, tiled=True)
    by_order = jnp.transpose(
        moved.reshape(moved.shape[0], moved.shape[1] * 6, orders), (2, 0, 1)
    )
    segment = lax.all_gather(legendre, "grp", axis=2, tiled=True)
    allowed = local_order_list[:, None] <= degree_list[None, :]
    table = jnp.where(allowed[:, None, :], segment, jnp.zeros_like(segment))
    latitudinal = lax.dot_general(
        table, by_order, (((2,), (1,)), ((0,), (0,))), preferred_element_type=F32
    ).astype(BF16)
    gathered = lax.all_to_all(latitudinal, "mem", split_axis=1, concat_axis=0, tiled=True)
    arranged = gathered.reshape(gathered.shape[0], gathered.shape[1], shells, 3, 2)
    trig = fourier_table(order_map, vorticity.shape[3])
    velocity = jnp.einsum("mtsck,mkp->tscp", arranged, trig, preferred_element_type=F32)
    return cross_product(velocity, vorticity)


MESH = pl.DeviceIdType.MESH
CHUNKS = ((0, 1), (2,))
SLOTS = 6


def transfers(bufs, sems, send_ref, place):
    from_sib, to_far, from_far, to_mem, recv = bufs
    grp, me, core, sibling, across = place
    sib_s, sib_r, far_s, far_r, mem_s, mem_r = sems

    def to_sibling(j):
        return pltpu.make_async_remote_copy(
            src_ref=send_ref.at[j, 1 - core], dst_ref=from_sib.at[j],
            send_sem=sib_s.at[j], recv_sem=sib_r.at[j],
            device_id=(sibling, me), device_id_type=MESH,
        )

    def to_across(j):
        return pltpu.make_async_remote_copy(
            src_ref=to_far.at[j], dst_ref=from_far.at[j],
            send_sem=far_s.at[j], recv_sem=far_r.at[j],
            device_id=(across, me), device_id_type=MESH,
        )

    def to_member(j, slot):
        return pltpu.make_async_remote_copy(
            src_ref=to_mem.at[j], dst_ref=recv.at[slot],
            send_sem=mem_s.at[j], recv_sem=mem_r.at[slot],
            device_id=(grp, j), device_id_type=MESH,
        )

    return to_sibling, to_across, to_member


def synth_body(
    groups, members, spec_hbm, inv_hbm, leg_hbm, deg_ref, ord_ref, *refs
):
    outs, refs = refs[: len(CHUNKS)], refs[len(CHUNKS) :]
    spec, inv, leg_ref, t0, t1, t2, main, rest, solved, f0, f1, f2, sems = refs[:13]
    refs = refs[13:]
    buffers = [refs[i * SLOTS : (i + 1) * SLOTS] for i in range(len(CHUNKS))]
    refs = refs[SLOTS * len(CHUNKS) :]
    sem_sets = [refs[i * 6 : (i + 1) * 6] for i in range(len(CHUNKS))]

    orders, radii, width = spec.shape[2:]
    shells = inv.shape[0]
    lats = leg_ref.shape[1]
    half = LANES // 2
    mine = shells // groups
    per_tile = LANES // orders
    pitch, lat_pitch = width + 1, orders + 1

    grp, me = lax.axis_index("grp"), lax.axis_index("mem")
    y, core = grp // 2, grp % 2
    sibling = y * 2 + (1 - core)
    across = (1 - y) * 2 + core
    place = (grp, me, core, sibling, across)

    barrier = pltpu.get_barrier_semaphore()
    for g in (sibling, across):
        pl.semaphore_signal(barrier, inc=1, device_id=(g, me), device_id_type=MESH)
    for i in range(1, members):
        pl.semaphore_signal(
            barrier, inc=1, device_id=(grp, (me + i) % members), device_id_type=MESH
        )

    pieces = 3 if shells % 6 == 0 else 1
    piece = shells // pieces
    inv_copies = [
        pltpu.make_async_copy(
            inv_hbm.at[pl.ds(i * piece, piece)], inv.at[pl.ds(i * piece, piece)], sems.at[4 + i]
        )
        for i in range(pieces)
    ]
    for copy in inv_copies:
        copy.start()
    copies = [pltpu.make_async_copy(spec_hbm.at[c], spec.at[c], sems.at[c]) for c in range(3)]
    leg_copy = pltpu.make_async_copy(leg_hbm, leg_ref, sems.at[3])
    for copy in (*copies, leg_copy):
        copy.start()

    eye = (
        lax.broadcasted_iota(jnp.int32, (2 * width, 2 * width), 0)
        == lax.broadcasted_iota(jnp.int32, (2 * width, 2 * width), 1)
    ).astype(BF16)

    def turn_inverse(i, carry):
        both = jnp.concatenate([inv[2 * i], inv[2 * i + 1]], axis=1)
        out = nt(eye, jnp.concatenate([both, both[LANES:]], axis=0))
        for h in range(2):
            at = pl.ds((2 * i + h) * pitch, width)
            part = out[h * width : (h + 1) * width]
            main[at, :] = part[:, 0:LANES]
            rest[at, :] = part[:, LANES : 2 * LANES]
        return carry

    for i, copy in enumerate(inv_copies):
        copy.wait()
        lax.fori_loop(i * piece // 2, (i + 1) * piece // 2, turn_inverse, 0, unroll=8)

    def turn(c):
        copies[c].wait()

        def turn_profiles(i, carry):
            stack = []
            for p in range(2):
                m = 4 * i + 2 * p
                a, b = [
                    jnp.concatenate([spec[c, k, m], spec[c, k, m + 1]], axis=1)
                    for k in range(2)
                ]
                stack += [a, b[LANES:], b[:LANES]]
            out = nt(eye, jnp.concatenate(stack, axis=0))
            for p in range(2):
                for h in range(2):
                    at = pl.ds((c * orders + 4 * i + 2 * p + h) * pitch, width)
                    part = out[h * width : (h + 1) * width]
                    for n, to in enumerate((t0, t1, t2)):
                        to[at, :] = part[:, (3 * p + n) * LANES : (3 * p + n + 1) * LANES]
            return carry

        lax.fori_loop(0, orders // 4, turn_profiles, 0, unroll=4)

    pad = jnp.zeros((half - shells, 2 * LANES), BF16)

    def solve_chunk(comps):
        count = len(comps) * orders
        low = lax.broadcasted_iota(jnp.int32, (count, LANES), 1) < half

        def solve(l, carry):
            at = pl.ds(comps[0] * orders * pitch + l, count, stride=pitch)
            shared = t1[at, :]
            real = jnp.concatenate([t0[at, :], jnp.where(low, shared, 0.0)], axis=1)
            imag = jnp.concatenate([t2[at, :], jnp.where(low, 0.0, shared)], axis=1)
            profiles = jnp.concatenate([real, imag], axis=0).astype(BF16)
            on = pl.ds(l, shells, stride=pitch)
            weights = jnp.concatenate([main[on, :], rest[on, :]], axis=1).astype(BF16)
            out = nt(profiles, jnp.concatenate([weights, pad], axis=0))
            solved[at, :] = jnp.concatenate([out[:count], out[count:]], axis=1)
            return carry

        lax.fori_loop(0, width, solve, 0, unroll=16)

    degrees = deg_ref[pl.ds(pl.multiple_of(grp * width, width), width)].reshape(1, width)
    sums = (f0, f1, f2)

    def sum_chunk(comps):
        def sum_degrees(m, carry):
            valid = degrees >= ord_ref[me * orders + m]
            table = jnp.where(valid, leg_ref[m].astype(F32), 0.0).astype(BF16)
            block = jnp.concatenate(
                [
                    solved[pl.ds((c * orders + m) * pitch, width), :].astype(BF16)
                    for c in comps
                ],
                axis=1,
            )
            out = nn(table, block)
            at = pl.ds(m, lats, stride=lat_pitch)
            for i, c in enumerate(comps):
                sums[c][at, :] = out[:, i * LANES : (i + 1) * LANES]
            return carry

        lax.fori_loop(0, orders, sum_degrees, 0, unroll=8)

    row = lax.broadcasted_iota(jnp.int32, (2 * shells, LANES), 0)
    lane = lax.broadcasted_iota(jnp.int32, (2 * shells, LANES), 1)
    want = row
    for i in range(1, 2 * groups):
        g, k = i // 2, i % 2
        step = (half + g * mine - i * mine) if k else (g * mine - i * mine)
        want = jnp.where(row >= i * mine, row + step, want)
    pick = (want == lane).astype(BF16)
    tiles = lats // members // per_tile

    def target(i):
        return (me + 1 + i) % members

    def pair_sum(n, j, which):
        send_ref, from_sib = buffers[n][:2]
        return send_ref[j, core, which].astype(F32) + from_sib[j, which].astype(F32)

    def send_chunk(n):
        send_ref, _, to_far = buffers[n][:3]
        to_sibling, to_across, _ = transfers(buffers[n][1:], sem_sets[n], send_ref, place)
        lag = 2

        def first(i):
            j = target(i)
            parts = []
            for b in range(tiles):
                at = [
                    pl.ds(((j * tiles + b) * per_tile + i) * lat_pitch, orders)
                    for i in range(per_tile)
                ]
                for c in CHUNKS[n]:
                    both = jnp.concatenate([sums[c][a, :].astype(BF16) for a in at], axis=0)
                    parts.append(nt(pick, both))
            for g in range(groups):
                block = [p[g * 2 * mine : (g + 1) * 2 * mine] for p in parts]
                send_ref[j, g % 2, g // 2] = jnp.concatenate(block, axis=0).astype(BF16)
            to_sibling(j).start()

        def second(i):
            j = target(i)
            to_sibling(j).wait_recv()
            to_far[j] = pair_sum(n, j, 1 - y).astype(BF16)
            to_across(j).start()

        def step(i, carry):
            first(i + lag)
            second(i)
            return carry

        for i in range(lag):
            first(i)
        lax.fori_loop(0, members - lag, step, 0)
        for i in range(members - lag, members):
            second(i)

    def third(n):
        _, to_across, to_member = transfers(buffers[n][1:], sem_sets[n], buffers[n][0], place)
        _, _, _, from_far, to_mem, _ = buffers[n]

        def total(j):
            to_across(j).wait_recv()
            return (pair_sum(n, j, y) + from_far[j].astype(F32)).astype(BF16)

        def step(i, carry):
            j = target(i)
            to_mem[j] = total(j)
            to_member(j, me).start()
            return carry

        lax.fori_loop(0, members - 1, step, 0)
        outs[n][me] = total(me)

    def finish(n):
        moves = transfers(buffers[n][1:], sem_sets[n], buffers[n][0], place)
        to_sibling, to_across, to_member = moves
        recv = buffers[n][5]

        def step(i, carry):
            j = target(i)
            to_member(j, j).wait_recv()
            outs[n][j] = recv[j]
            to_member(j, me).wait_send()
            return carry

        lax.fori_loop(0, members - 1, step, 0)

        def drain(i, carry):
            to_sibling(i).wait_send()
            to_across(i).wait_send()
            return carry

        lax.fori_loop(0, members, drain, 0)

    last = len(CHUNKS) - 1
    for n, comps in enumerate(CHUNKS):
        for c in comps:
            turn(c)
        solve_chunk(comps)
        if n:
            third(n - 1)
        if n == 0:
            leg_copy.wait()
        sum_chunk(comps)
        if n == 0:
            pl.semaphore_wait(barrier, members + 1)
        send_chunk(n)
    third(last)
    for n in range(len(CHUNKS)):
        finish(n)


def synthesize(spec, inv, legendre, degree_list, order_map, groups, members):
    _, _, orders, radii, width = spec.shape
    shells = inv.shape[0]
    lats = legendre.shape[1]
    mine = shells // groups
    pitch = width + 1
    any_space = pl.BlockSpec(memory_space=pl.ANY)
    vmem = pl.BlockSpec(memory_space=pltpu.VMEM)
    buffers, shapes = [], []
    for comps in CHUNKS:
        block = lats // members * orders * mine * 2 * len(comps) // LANES
        slots = pltpu.VMEM((members, block, LANES), BF16)
        buffers += [
            pltpu.VMEM((members, 2, groups // 2, block, LANES), BF16),
            pltpu.VMEM((members, groups // 2, block, LANES), BF16),
            slots, slots, slots, slots,
        ]
        shapes.append(jax.ShapeDtypeStruct((members, block, LANES), BF16))
    return pl.pallas_call(
        functools.partial(synth_body, groups, members),
        out_shape=shapes,
        in_specs=[any_space] * 3 + [vmem, pl.BlockSpec(memory_space=pltpu.SMEM)],
        out_specs=[vmem] * len(CHUNKS),
        scratch_shapes=[
            pltpu.VMEM(spec.shape, BF16),
            pltpu.VMEM(inv.shape, BF16),
            pltpu.VMEM(legendre.shape, BF16),
            *[pltpu.VMEM((3 * orders * pitch, LANES), F32)] * 3,
            *[pltpu.VMEM((shells * pitch, LANES), F32)] * 2,
            pltpu.VMEM((3 * orders * pitch, LANES), F32),
            *[pltpu.VMEM((lats * (orders + 1), LANES), F32)] * 3,
            pltpu.SemaphoreType.DMA((7,)),
            *buffers,
            *[pltpu.SemaphoreType.DMA((members,))] * (6 * len(CHUNKS)),
        ],
        compiler_params=pltpu.CompilerParams(
            collective_id=0, has_side_effects=True, vmem_limit_bytes=60 * 2**20
        ),
        name="synthesize",
    )(spec, inv, legendre, degree_list, order_map)


def cos_sin(phase, count):
    phase = phase - count * jnp.floor((phase + 0.5) * (1.0 / count))
    turns = jnp.floor((phase + count / 8) * (4.0 / count))
    t = (phase - turns * (count / 4)) * (2.0 * math.pi / count)
    x = t * t
    s = t * (1 + x * (-1 / 6 + x * (1 / 120 + x * (-1 / 5040 + x * (1 / 362880)))))
    c = 1 + x * (
        -1 / 2 + x * (1 / 24 + x * (-1 / 720 + x * (1 / 40320 + x * (-1 / 3628800))))
    )
    odd = (turns == 1) | (turns == 3)
    cos, sin = jnp.where(odd, s, c), jnp.where(odd, c, s)
    cos = jnp.where((turns == 1) | (turns == 2), -cos, cos)
    sin = jnp.where((turns == 2) | (turns == 3), -sin, sin)
    return cos, sin


def physical_body(orders, *refs):
    recvs, refs = refs[: len(CHUNKS)], refs[len(CHUNKS) :]
    vort_hbm, ord_ref, out_ref, vort_ref, sem, *keep = refs
    held, keep = keep[: len(CHUNKS)], keep[len(CHUNKS) :]
    copy = pltpu.make_async_copy(vort_hbm, vort_ref, sem.at[0])
    arrivals = [
        pltpu.make_async_copy(r, h, sem.at[1 + n]) for n, (r, h) in enumerate(zip(recvs, held))
    ]
    for arrival in arrivals:
        arrival.start()
    copy.start()
    members = recvs[0].shape[0]
    shells = vort_ref.shape[1]
    lats = vort_ref.shape[2]
    points = vort_ref.shape[3]
    every = members * orders
    per_tile = LANES // orders
    tiles = lats // per_tile
    line = ord_ref[...].reshape(1, every).astype(F32)
    same = lax.broadcasted_iota(jnp.int32, (every, every), 0) == lax.broadcasted_iota(
        jnp.int32, (every, every), 1
    )
    column = jnp.sum(jnp.where(same, line, 0.0), axis=1, keepdims=True)
    lane = lax.broadcasted_iota(jnp.int32, (every, LANES), 1).astype(F32)
    nc, ns = cos_sin(column * lane, points)
    weight = jnp.where(column == 0.0, 1.0, 2.0)
    nc, ns = weight * nc, weight * ns
    far_c, far_s = cos_sin(column * (lane * LANES), points)

    for arrival in arrivals:
        arrival.wait()
    for comps, recv_ref in zip(CHUNKS, held):
        for i in range(per_tile):
            for h in range(members // per_tile):
                parts = [
                    recv_ref[h * per_tile + j].astype(F32)[:, i * orders : (i + 1) * orders]
                    for j in range(per_tile)
                ]
                joined = jnp.concatenate(parts, axis=1)
                for b in range(tiles):
                    for n, c in enumerate(comps):
                        for k in range(2):
                            at = ((b * len(comps) + n) * 2 + k) * shells
                            to = pl.ds(
                                c * shells * lats + b * per_tile + i, shells, stride=lats
                            )
                            keep[k * (members // per_tile) + h][to, :] = joined[at : at + shells]
    left = jnp.concatenate([r[...].astype(BF16) for r in keep], axis=1)

    flat = shells * lats
    copy.wait()
    for q in range(points // LANES):
        on = slice(q * LANES, (q + 1) * LANES)
        fc, fs = far_c[:, q : q + 1], far_s[:, q : q + 1]
        trig = jnp.concatenate([nc * fc - ns * fs, -(ns * fc + nc * fs)], axis=0).astype(BF16)
        v = nn(left, trig)
        v0, v1, v2 = v[:flat], v[flat : 2 * flat], v[2 * flat :]
        w0, w1, w2 = [vort_ref[c, :, :, on].reshape(flat, LANES).astype(F32) for c in range(3)]
        shape = (shells, lats, LANES)
        out_ref[0, :, :, on] = (v1 * w2 - v2 * w1).astype(BF16).reshape(shape)
        out_ref[1, :, :, on] = (v2 * w0 - v0 * w2).astype(BF16).reshape(shape)
        out_ref[2, :, :, on] = (v0 * w1 - v1 * w0).astype(BF16).reshape(shape)


def physical(received, vorticity, order_map, orders):
    members = received[0].shape[0]
    _, shells, lats, _ = vorticity.shape
    vmem = pl.BlockSpec(memory_space=pltpu.VMEM)
    return pl.pallas_call(
        functools.partial(physical_body, orders),
        out_shape=jax.ShapeDtypeStruct(vorticity.shape, BF16),
        in_specs=[pl.BlockSpec(memory_space=pl.ANY)] * (len(CHUNKS) + 1) + [vmem],
        out_specs=vmem,
        scratch_shapes=[
            pltpu.VMEM(vorticity.shape, BF16),
            pltpu.SemaphoreType.DMA((1 + len(CHUNKS),)),
        ]
        + [pltpu.VMEM(r.shape, BF16) for r in received]
        + [pltpu.VMEM((3 * shells * lats, LANES), F32)] * (2 * members * orders // LANES),
        compiler_params=pltpu.CompilerParams(vmem_limit_bytes=60 * 2**20),
        name="physical",
    )(*received, vorticity, order_map)


def shards(groups, members, spectral, inverse, legendre, vorticity, degree_list, order_map):
    orders = spectral.shape[3]
    spec = jnp.transpose(spectral, (1, 2, 3, 4, 0))
    inv = jnp.transpose(inverse, (1, 2, 0))
    vort = jnp.transpose(vorticity, (0, 2, 1, 3))
    received = synthesize(spec, inv, legendre, degree_list, order_map, groups, members)
    out = physical(received, vort, order_map, orders)
    return jnp.transpose(out, (0, 2, 1, 3))


def solution(mesh):
    groups, members = mesh.shape["grp"], mesh.shape["mem"]

    def local(spectral, inverse, legendre, vorticity, degree_list, order_map):
        args = (spectral, inverse, legendre, vorticity, degree_list, order_map)
        width, _, _, orders, radii = spectral.shape
        shells, lats = inverse.shape[1], legendre.shape[1]
        fits = (
            groups == 4
            and width == LANES
            and 2 * shells <= LANES
            and LANES < radii
            and 2 * radii == 3 * LANES
            and LANES % orders == 0
            and orders % 4 == 0
            and shells % 2 == 0
            and (shells // groups * 2) % 8 == 0
            and members % (LANES // orders) == 0
            and (lats // members) % (LANES // orders) == 0
            and vorticity.shape[3] % LANES == 0
            and vorticity.shape[3] // LANES <= LANES
            and members * orders * vorticity.shape[3] < 2**23
            and (lats // members) * orders * (shells // groups) * 2 % (16 * LANES) == 0
        )
        if fits:
            return shards(groups, members, *args)
        return plain_shards(*args)

    return jax.shard_map(
        local,
        mesh=mesh,
        in_specs=(
            P("grp", None, None, "mem", None),
            P("grp", None, None),
            P("mem", None, "grp"),
            P(None, "mem", "grp", None),
            P(),
            P(),
        ),
        out_specs=P(None, "mem", "grp", None),
        check_vma=False,
    )
```

```python
import functools
import math

import jax
import jax.numpy as jnp
from jax import lax
from jax.experimental import pallas as pl
from jax.experimental.pallas import tpu as pltpu
from jax.sharding import PartitionSpec as P

F32 = jnp.float32
BF16 = jnp.bfloat16
LANES = 128
NT = (((1,), (1,)), ((), ()))
NN = (((1,), (0,)), ((), ()))


def nt(a, b):
    return lax.dot_general(a, b, NT, preferred_element_type=F32)


def nn(a, b):
    return lax.dot_general(a, b, NN, preferred_element_type=F32)


def cross_product(flow_velocity, vorticity):
    other = vorticity.astype(jnp.float32)
    first = flow_velocity[:, :, 1] * other[2] - flow_velocity[:, :, 2] * other[1]
    second = flow_velocity[:, :, 2] * other[0] - flow_velocity[:, :, 0] * other[2]
    third = flow_velocity[:, :, 0] * other[1] - flow_velocity[:, :, 1] * other[0]
    return jnp.stack([first, second, third]).astype(jnp.bfloat16)


def fourier_table(order_map, count):
    longitude = jnp.arange(count, dtype=jnp.int32)
    phase = order_map[:, None] * longitude[None, :] % count
    angle = phase.astype(jnp.float32) * (2.0 * math.pi / count)
    weight = jnp.where(order_map == 0, 1.0, 2.0).astype(jnp.float32)[:, None]
    return jnp.stack([weight * jnp.cos(angle), -weight * jnp.sin(angle)], axis=1).astype(
        jnp.bfloat16
    )


def plain_shards(spectral, inverse, legendre, vorticity, degree_list, order_map):
    orders = spectral.shape[3]
    shells = vorticity.shape[2]
    local_order_list = lax.dynamic_slice_in_dim(
        order_map, lax.axis_index("mem") * orders, orders
    )
    width = spectral.shape[0]
    flat = spectral.reshape(width, 6 * orders, spectral.shape[4])
    solved = lax.dot_general(
        inverse, flat, (((2,), (2,)), ((0,), (0,))), preferred_element_type=F32
    ).astype(BF16)
    moved = lax.all_to_all(solved, "grp", split_axis=1, concat_axis=0, tiled=True)
    by_order = jnp.transpose(
        moved.reshape(moved.shape[0], moved.shape[1] * 6, orders), (2, 0, 1)
    )
    segment = lax.all_gather(legendre, "grp", axis=2, tiled=True)
    allowed = local_order_list[:, None] <= degree_list[None, :]
    table = jnp.where(allowed[:, None, :], segment, jnp.zeros_like(segment))
    latitudinal = lax.dot_general(
        table, by_order, (((2,), (1,)), ((0,), (0,))), preferred_element_type=F32
    ).astype(BF16)
    gathered = lax.all_to_all(latitudinal, "mem", split_axis=1, concat_axis=0, tiled=True)
    arranged = gathered.reshape(gathered.shape[0], gathered.shape[1], shells, 3, 2)
    trig = fourier_table(order_map, vorticity.shape[3])
    velocity = jnp.einsum("mtsck,mkp->tscp", arranged, trig, preferred_element_type=F32)
    return cross_product(velocity, vorticity)


MESH = pl.DeviceIdType.MESH
CHUNKS = ((0, 1), (2,))
SLOTS = 6


def transfers(bufs, sems, send_ref, place):
    from_sib, to_far, from_far, to_mem, recv = bufs
    grp, me, core, sibling, across = place
    sib_s, sib_r, far_s, far_r, mem_s, mem_r = sems

    def to_sibling(j):
        return pltpu.make_async_remote_copy(
            src_ref=send_ref.at[j, 1 - core], dst_ref=from_sib.at[j],
            send_sem=sib_s.at[j], recv_sem=sib_r.at[j],
            device_id=(sibling, me), device_id_type=MESH,
        )

    def to_across(j):
        return pltpu.make_async_remote_copy(
            src_ref=to_far.at[j], dst_ref=from_far.at[j],
            send_sem=far_s.at[j], recv_sem=far_r.at[j],
            device_id=(across, me), device_id_type=MESH,
        )

    def to_member(j, slot):
        return pltpu.make_async_remote_copy(
            src_ref=to_mem.at[j], dst_ref=recv.at[slot],
            send_sem=mem_s.at[j], recv_sem=mem_r.at[slot],
            device_id=(grp, j), device_id_type=MESH,
        )

    return to_sibling, to_across, to_member


def synth_body(
    groups, members, spec_hbm, inv_hbm, leg_hbm, deg_ref, ord_ref, *refs
):
    outs, refs = refs[: len(CHUNKS)], refs[len(CHUNKS) :]
    spec, inv, leg_ref, t0, t1, t2, main, rest, solved, f0, f1, f2, sems = refs[:13]
    refs = refs[13:]
    buffers = [refs[i * SLOTS : (i + 1) * SLOTS] for i in range(len(CHUNKS))]
    refs = refs[SLOTS * len(CHUNKS) :]
    sem_sets = [refs[i * 6 : (i + 1) * 6] for i in range(len(CHUNKS))]

    orders, radii, width = spec.shape[2:]
    shells = inv.shape[0]
    lats = leg_ref.shape[1]
    half = LANES // 2
    mine = shells // groups
    per_tile = LANES // orders
    pitch, lat_pitch = width + 1, orders + 1

    grp, me = lax.axis_index("grp"), lax.axis_index("mem")
    y, core = grp // 2, grp % 2
    sibling = y * 2 + (1 - core)
    across = (1 - y) * 2 + core
    place = (grp, me, core, sibling, across)

    barrier = pltpu.get_barrier_semaphore()
    for g in (sibling, across):
        pl.semaphore_signal(barrier, inc=1, device_id=(g, me), device_id_type=MESH)
    for i in range(1, members):
        pl.semaphore_signal(
            barrier, inc=1, device_id=(grp, (me + i) % members), device_id_type=MESH
        )

    pieces = 3 if shells % 6 == 0 else 1
    piece = shells // pieces
    inv_copies = [
        pltpu.make_async_copy(
            inv_hbm.at[pl.ds(i * piece, piece)], inv.at[pl.ds(i * piece, piece)], sems.at[4 + i]
        )
        for i in range(pieces)
    ]
    for copy in inv_copies:
        copy.start()
    copies = [pltpu.make_async_copy(spec_hbm.at[c], spec.at[c], sems.at[c]) for c in range(3)]
    leg_copy = pltpu.make_async_copy(leg_hbm, leg_ref, sems.at[3])
    for copy in (*copies, leg_copy):
        copy.start()

    eye = (
        lax.broadcasted_iota(jnp.int32, (2 * width, 2 * width), 0)
        == lax.broadcasted_iota(jnp.int32, (2 * width, 2 * width), 1)
    ).astype(BF16)

    def turn_inverse(i, carry):
        both = jnp.concatenate([inv[2 * i], inv[2 * i + 1]], axis=1)
        out = nt(eye, jnp.concatenate([both, both[LANES:]], axis=0))
        for h in range(2):
            at = pl.ds((2 * i + h) * pitch, width)
            part = out[h * width : (h + 1) * width]
            main[at, :] = part[:, 0:LANES]
            rest[at, :] = part[:, LANES : 2 * LANES]
        return carry

    for i, copy in enumerate(inv_copies):
        copy.wait()
        lax.fori_loop(i * piece // 2, (i + 1) * piece // 2, turn_inverse, 0, unroll=8)

    def turn(c):
        copies[c].wait()

        def turn_profiles(i, carry):
            stack = []
            for p in range(2):
                m = 4 * i + 2 * p
                a, b = [
                    jnp.concatenate([spec[c, k, m], spec[c, k, m + 1]], axis=1)
                    for k in range(2)
                ]
                stack += [a, b[LANES:], b[:LANES]]
            out = nt(eye, jnp.concatenate(stack, axis=0))
            for p in range(2):
                for h in range(2):
                    at = pl.ds((c * orders + 4 * i + 2 * p + h) * pitch, width)
                    part = out[h * width : (h + 1) * width]
                    for n, to in enumerate((t0, t1, t2)):
                        to[at, :] = part[:, (3 * p + n) * LANES : (3 * p + n + 1) * LANES]
            return carry

        lax.fori_loop(0, orders // 4, turn_profiles, 0, unroll=4)

    pad = jnp.zeros((half - shells, 2 * LANES), BF16)

    def solve_chunk(comps):
        count = len(comps) * orders
        low = lax.broadcasted_iota(jnp.int32, (count, LANES), 1) < half

        def solve(l, carry):
            at = pl.ds(comps[0] * orders * pitch + l, count, stride=pitch)
            shared = t1[at, :]
            real = jnp.concatenate([t0[at, :], jnp.where(low, shared, 0.0)], axis=1)
            imag = jnp.concatenate([t2[at, :], jnp.where(low, 0.0, shared)], axis=1)
            profiles = jnp.concatenate([real, imag], axis=0).astype(BF16)
            on = pl.ds(l, shells, stride=pitch)
            weights = jnp.concatenate([main[on, :], rest[on, :]], axis=1).astype(BF16)
            out = nt(profiles, jnp.concatenate([weights, pad], axis=0))
            solved[at, :] = jnp.concatenate([out[:count], out[count:]], axis=1)
            return carry

        lax.fori_loop(0, width, solve, 0, unroll=16)

    degrees = deg_ref[pl.ds(pl.multiple_of(grp * width, width), width)].reshape(1, width)
    sums = (f0, f1, f2)

    def sum_chunk(comps):
        def sum_degrees(m, carry):
            valid = degrees >= ord_ref[me * orders + m]
            table = jnp.where(valid, leg_ref[m].astype(F32), 0.0).astype(BF16)
            block = jnp.concatenate(
                [
                    solved[pl.ds((c * orders + m) * pitch, width), :].astype(BF16)
                    for c in comps
                ],
                axis=1,
            )
            out = nn(table, block)
            at = pl.ds(m, lats, stride=lat_pitch)
            for i, c in enumerate(comps):
                sums[c][at, :] = out[:, i * LANES : (i + 1) * LANES]
            return carry

        lax.fori_loop(0, orders, sum_degrees, 0, unroll=8)

    row = lax.broadcasted_iota(jnp.int32, (2 * shells, LANES), 0)
    lane = lax.broadcasted_iota(jnp.int32, (2 * shells, LANES), 1)
    want = row
    for i in range(1, 2 * groups):
        g, k = i // 2, i % 2
        step = (half + g * mine - i * mine) if k else (g * mine - i * mine)
        want = jnp.where(row >= i * mine, row + step, want)
    pick = (want == lane).astype(BF16)
    tiles = lats // members // per_tile

    def target(i):
        return (me + 1 + i) % members

    def pair_sum(n, j, which):
        send_ref, from_sib = buffers[n][:2]
        return send_ref[j, core, which].astype(F32) + from_sib[j, which].astype(F32)

    def send_chunk(n):
        send_ref, _, to_far = buffers[n][:3]
        to_sibling, to_across, _ = transfers(buffers[n][1:], sem_sets[n], send_ref, place)
        lag = 2

        def first(i):
            j = target(i)
            parts = []
            for b in range(tiles):
                at = [
                    pl.ds(((j * tiles + b) * per_tile + i) * lat_pitch, orders)
                    for i in range(per_tile)
                ]
                for c in CHUNKS[n]:
                    both = jnp.concatenate([sums[c][a, :].astype(BF16) for a in at], axis=0)
                    parts.append(nt(pick, both))
            for g in range(groups):
                block = [p[g * 2 * mine : (g + 1) * 2 * mine] for p in parts]
                send_ref[j, g % 2, g // 2] = jnp.concatenate(block, axis=0).astype(BF16)
            to_sibling(j).start()

        def second(i):
            j = target(i)
            to_sibling(j).wait_recv()
            to_far[j] = pair_sum(n, j, 1 - y).astype(BF16)
            to_across(j).start()

        def step(i, carry):
            first(i + lag)
            second(i)
            return carry

        for i in range(lag):
            first(i)
        lax.fori_loop(0, members - lag, step, 0)
        for i in range(members - lag, members):
            second(i)

    def third(n):
        _, to_across, to_member = transfers(buffers[n][1:], sem_sets[n], buffers[n][0], place)
        _, _, _, from_far, to_mem, _ = buffers[n]

        def total(j):
            to_across(j).wait_recv()
            return (pair_sum(n, j, y) + from_far[j].astype(F32)).astype(BF16)

        def step(i, carry):
            j = target(i)
            to_mem[j] = total(j)
            to_member(j, me).start()
            return carry

        lax.fori_loop(0, members - 1, step, 0)
        outs[n][me] = total(me)

    def finish(n):
        moves = transfers(buffers[n][1:], sem_sets[n], buffers[n][0], place)
        to_sibling, to_across, to_member = moves
        recv = buffers[n][5]

        def step(i, carry):
            j = target(i)
            to_member(j, j).wait_recv()
            outs[n][j] = recv[j]
            to_member(j, me).wait_send()
            return carry

        lax.fori_loop(0, members - 1, step, 0)

        def drain(i, carry):
            to_sibling(i).wait_send()
            to_across(i).wait_send()
            return carry

        lax.fori_loop(0, members, drain, 0)

    last = len(CHUNKS) - 1
    for n, comps in enumerate(CHUNKS):
        for c in comps:
            turn(c)
        solve_chunk(comps)
        if n == 0:
            leg_copy.wait()
        sum_chunk(comps)
        if n:
            third(n - 1)
        if n == 0:
            pl.semaphore_wait(barrier, members + 1)
        send_chunk(n)
    third(last)
    for n in range(len(CHUNKS)):
        finish(n)


def synthesize(spec, inv, legendre, degree_list, order_map, groups, members):
    _, _, orders, radii, width = spec.shape
    shells = inv.shape[0]
    lats = legendre.shape[1]
    mine = shells // groups
    pitch = width + 1
    any_space = pl.BlockSpec(memory_space=pl.ANY)
    vmem = pl.BlockSpec(memory_space=pltpu.VMEM)
    buffers, shapes = [], []
    for comps in CHUNKS:
        block = lats // members * orders * mine * 2 * len(comps) // LANES
        slots = pltpu.VMEM((members, block, LANES), BF16)
        buffers += [
            pltpu.VMEM((members, 2, groups // 2, block, LANES), BF16),
            pltpu.VMEM((members, groups // 2, block, LANES), BF16),
            slots, slots, slots, slots,
        ]
        shapes.append(jax.ShapeDtypeStruct((members, block, LANES), BF16))
    return pl.pallas_call(
        functools.partial(synth_body, groups, members),
        out_shape=shapes,
        in_specs=[any_space] * 3 + [vmem, pl.BlockSpec(memory_space=pltpu.SMEM)],
        out_specs=[vmem] * len(CHUNKS),
        scratch_shapes=[
            pltpu.VMEM(spec.shape, BF16),
            pltpu.VMEM(inv.shape, BF16),
            pltpu.VMEM(legendre.shape, BF16),
            *[pltpu.VMEM((3 * orders * pitch, LANES), F32)] * 3,
            *[pltpu.VMEM((shells * pitch, LANES), F32)] * 2,
            pltpu.VMEM((3 * orders * pitch, LANES), F32),
            *[pltpu.VMEM((lats * (orders + 1), LANES), F32)] * 3,
            pltpu.SemaphoreType.DMA((7,)),
            *buffers,
            *[pltpu.SemaphoreType.DMA((members,))] * (6 * len(CHUNKS)),
        ],
        compiler_params=pltpu.CompilerParams(
            collective_id=0, has_side_effects=True, vmem_limit_bytes=60 * 2**20
        ),
        name="synthesize",
    )(spec, inv, legendre, degree_list, order_map)


def cos_sin(phase, count):
    phase = phase - count * jnp.floor((phase + 0.5) * (1.0 / count))
    turns = jnp.floor((phase + count / 8) * (4.0 / count))
    t = (phase - turns * (count / 4)) * (2.0 * math.pi / count)
    x = t * t
    s = t * (1 + x * (-1 / 6 + x * (1 / 120 + x * (-1 / 5040 + x * (1 / 362880)))))
    c = 1 + x * (
        -1 / 2 + x * (1 / 24 + x * (-1 / 720 + x * (1 / 40320 + x * (-1 / 3628800))))
    )
    odd = (turns == 1) | (turns == 3)
    cos, sin = jnp.where(odd, s, c), jnp.where(odd, c, s)
    cos = jnp.where((turns == 1) | (turns == 2), -cos, cos)
    sin = jnp.where((turns == 2) | (turns == 3), -sin, sin)
    return cos, sin


def physical_body(orders, wide, *refs):
    recvs, refs = refs[: len(CHUNKS)], refs[len(CHUNKS) :]
    vort_hbm, ord_ref, out_hbm, vort_ref, made, sem, *keep = refs
    held, keep = keep[: len(CHUNKS)], keep[len(CHUNKS) :]
    copy = pltpu.make_async_copy(vort_hbm, vort_ref, sem.at[0])
    arrivals = [
        pltpu.make_async_copy(r, h, sem.at[1 + n]) for n, (r, h) in enumerate(zip(recvs, held))
    ]
    for arrival in arrivals:
        arrival.start()
    copy.start()
    members = recvs[0].shape[0]
    shells = vort_ref.shape[1]
    lats = vort_ref.shape[2]
    points = vort_ref.shape[3]
    every = members * orders
    per_tile = LANES // orders
    tiles = lats // per_tile
    line = ord_ref[...].reshape(1, every).astype(F32)
    same = lax.broadcasted_iota(jnp.int32, (every, every), 0) == lax.broadcasted_iota(
        jnp.int32, (every, every), 1
    )
    column = jnp.sum(jnp.where(same, line, 0.0), axis=1, keepdims=True)
    lane = lax.broadcasted_iota(jnp.int32, (every, LANES), 1).astype(F32)
    nc, ns = cos_sin(column * lane, points)
    weight = jnp.where(column == 0.0, 1.0, 2.0)
    nc, ns = weight * nc, weight * ns
    far_c, far_s = cos_sin(column * (lane * LANES), points)

    for arrival in arrivals:
        arrival.wait()
    for comps, recv_ref in zip(CHUNKS, held):
        for i in range(per_tile):
            for h in range(members // per_tile):
                parts = [
                    recv_ref[h * per_tile + j].astype(F32)[:, i * orders : (i + 1) * orders]
                    for j in range(per_tile)
                ]
                joined = jnp.concatenate(parts, axis=1)
                for b in range(tiles):
                    for n, c in enumerate(comps):
                        for k in range(2):
                            at = ((b * len(comps) + n) * 2 + k) * shells
                            to = pl.ds(
                                c * shells * lats + b * per_tile + i, shells, stride=lats
                            )
                            keep[k * (members // per_tile) + h][to, :] = joined[at : at + shells]
    left = jnp.concatenate([r[...].astype(BF16) for r in keep], axis=1)

    flat = shells * lats
    shape = (shells, lats, wide)
    copy.wait()
    writes = []
    for q in range(points // wide):
        on = pl.ds(q * wide, wide)
        tables = []
        for p in range(q * wide // LANES, (q + 1) * wide // LANES):
            fc, fs = far_c[:, p : p + 1], far_s[:, p : p + 1]
            tables.append(jnp.concatenate([nc * fc - ns * fs, -(ns * fc + nc * fs)], axis=0))
        v = nn(left, jnp.concatenate(tables, axis=1).astype(BF16))
        v0, v1, v2 = v[:flat], v[flat : 2 * flat], v[2 * flat :]
        w0, w1, w2 = [vort_ref[c, :, :, on].reshape(flat, wide).astype(F32) for c in range(3)]
        made[0, :, :, on] = (v1 * w2 - v2 * w1).astype(BF16).reshape(shape)
        made[1, :, :, on] = (v2 * w0 - v0 * w2).astype(BF16).reshape(shape)
        made[2, :, :, on] = (v0 * w1 - v1 * w0).astype(BF16).reshape(shape)
        writes.append(
            pltpu.make_async_copy(
                made.at[:, :, :, on], out_hbm.at[:, :, :, on], sem.at[1 + len(CHUNKS) + q]
            )
        )
        writes[-1].start()
    for write in writes:
        write.wait()


def physical(received, vorticity, order_map, orders):
    members = received[0].shape[0]
    _, shells, lats, points = vorticity.shape
    wide = 2 * LANES if points % (2 * LANES) == 0 else LANES
    vmem = pl.BlockSpec(memory_space=pltpu.VMEM)
    return pl.pallas_call(
        functools.partial(physical_body, orders, wide),
        out_shape=jax.ShapeDtypeStruct(vorticity.shape, BF16),
        in_specs=[pl.BlockSpec(memory_space=pl.ANY)] * (len(CHUNKS) + 1) + [vmem],
        out_specs=pl.BlockSpec(memory_space=pl.ANY),
        scratch_shapes=[
            pltpu.VMEM(vorticity.shape, BF16),
            pltpu.VMEM(vorticity.shape, BF16),
            pltpu.SemaphoreType.DMA((1 + len(CHUNKS) + points // wide,)),
        ]
        + [pltpu.VMEM(r.shape, BF16) for r in received]
        + [pltpu.VMEM((3 * shells * lats, LANES), F32)] * (2 * members * orders // LANES),
        compiler_params=pltpu.CompilerParams(vmem_limit_bytes=60 * 2**20),
        name="physical",
    )(*received, vorticity, order_map)


def shards(groups, members, spectral, inverse, legendre, vorticity, degree_list, order_map):
    orders = spectral.shape[3]
    spec = jnp.transpose(spectral, (1, 2, 3, 4, 0))
    inv = jnp.transpose(inverse, (1, 2, 0))
    vort = jnp.transpose(vorticity, (0, 2, 1, 3))
    received = synthesize(spec, inv, legendre, degree_list, order_map, groups, members)
    out = physical(received, vort, order_map, orders)
    return jnp.transpose(out, (0, 2, 1, 3))


def solution(mesh):
    groups, members = mesh.shape["grp"], mesh.shape["mem"]

    def local(spectral, inverse, legendre, vorticity, degree_list, order_map):
        args = (spectral, inverse, legendre, vorticity, degree_list, order_map)
        width, _, _, orders, radii = spectral.shape
        shells, lats = inverse.shape[1], legendre.shape[1]
        fits = (
            groups == 4
            and width == LANES
            and 2 * shells <= LANES
            and LANES < radii
            and 2 * radii == 3 * LANES
            and LANES % orders == 0
            and orders % 4 == 0
            and shells % 2 == 0
            and (shells // groups * 2) % 8 == 0
            and members % (LANES // orders) == 0
            and (lats // members) % (LANES // orders) == 0
            and vorticity.shape[3] % LANES == 0
            and vorticity.shape[3] // LANES <= LANES
            and members * orders * vorticity.shape[3] < 2**23
            and (lats // members) * orders * (shells // groups) * 2 % (16 * LANES) == 0
        )
        if fits:
            return shards(groups, members, *args)
        return plain_shards(*args)

    return jax.shard_map(
        local,
        mesh=mesh,
        in_specs=(
            P("grp", None, None, "mem", None),
            P("grp", None, None),
            P("mem", None, "grp"),
            P(None, "mem", "grp", None),
            P(),
            P(),
        ),
        out_specs=P(None, "mem", "grp", None),
        check_vma=False,
    )
```

```python
import functools
import math

import jax
import jax.numpy as jnp
from jax import lax
from jax.experimental import pallas as pl
from jax.experimental.pallas import tpu as pltpu
from jax.sharding import PartitionSpec as P

F32 = jnp.float32
BF16 = jnp.bfloat16
LANES = 128
NT = (((1,), (1,)), ((), ()))
NN = (((1,), (0,)), ((), ()))


def nt(a, b):
    return lax.dot_general(a, b, NT, preferred_element_type=F32)


def nn(a, b):
    return lax.dot_general(a, b, NN, preferred_element_type=F32)


def cross_product(flow_velocity, vorticity):
    other = vorticity.astype(jnp.float32)
    first = flow_velocity[:, :, 1] * other[2] - flow_velocity[:, :, 2] * other[1]
    second = flow_velocity[:, :, 2] * other[0] - flow_velocity[:, :, 0] * other[2]
    third = flow_velocity[:, :, 0] * other[1] - flow_velocity[:, :, 1] * other[0]
    return jnp.stack([first, second, third]).astype(jnp.bfloat16)


def fourier_table(order_map, count):
    longitude = jnp.arange(count, dtype=jnp.int32)
    phase = order_map[:, None] * longitude[None, :] % count
    angle = phase.astype(jnp.float32) * (2.0 * math.pi / count)
    weight = jnp.where(order_map == 0, 1.0, 2.0).astype(jnp.float32)[:, None]
    return jnp.stack([weight * jnp.cos(angle), -weight * jnp.sin(angle)], axis=1).astype(
        jnp.bfloat16
    )


def plain_shards(spectral, inverse, legendre, vorticity, degree_list, order_map):
    orders = spectral.shape[3]
    shells = vorticity.shape[2]
    local_order_list = lax.dynamic_slice_in_dim(
        order_map, lax.axis_index("mem") * orders, orders
    )
    width = spectral.shape[0]
    flat = spectral.reshape(width, 6 * orders, spectral.shape[4])
    solved = lax.dot_general(
        inverse, flat, (((2,), (2,)), ((0,), (0,))), preferred_element_type=F32
    ).astype(BF16)
    moved = lax.all_to_all(solved, "grp", split_axis=1, concat_axis=0, tiled=True)
    by_order = jnp.transpose(
        moved.reshape(moved.shape[0], moved.shape[1] * 6, orders), (2, 0, 1)
    )
    segment = lax.all_gather(legendre, "grp", axis=2, tiled=True)
    allowed = local_order_list[:, None] <= degree_list[None, :]
    table = jnp.where(allowed[:, None, :], segment, jnp.zeros_like(segment))
    latitudinal = lax.dot_general(
        table, by_order, (((2,), (1,)), ((0,), (0,))), preferred_element_type=F32
    ).astype(BF16)
    gathered = lax.all_to_all(latitudinal, "mem", split_axis=1, concat_axis=0, tiled=True)
    arranged = gathered.reshape(gathered.shape[0], gathered.shape[1], shells, 3, 2)
    trig = fourier_table(order_map, vorticity.shape[3])
    velocity = jnp.einsum("mtsck,mkp->tscp", arranged, trig, preferred_element_type=F32)
    return cross_product(velocity, vorticity)


MESH = pl.DeviceIdType.MESH
CHUNKS = ((0, 1), (2,))
SLOTS = 6


def transfers(bufs, sems, send_ref, place):
    from_sib, to_far, from_far, to_mem, recv = bufs
    grp, me, core, sibling, across = place
    sib_s, sib_r, far_s, far_r, mem_s, mem_r = sems

    def to_sibling(j):
        return pltpu.make_async_remote_copy(
            src_ref=send_ref.at[j, 1 - core], dst_ref=from_sib.at[j],
            send_sem=sib_s.at[j], recv_sem=sib_r.at[j],
            device_id=(sibling, me), device_id_type=MESH,
        )

    def to_across(j):
        return pltpu.make_async_remote_copy(
            src_ref=to_far.at[j], dst_ref=from_far.at[j],
            send_sem=far_s.at[j], recv_sem=far_r.at[j],
            device_id=(across, me), device_id_type=MESH,
        )

    def to_member(j, slot):
        return pltpu.make_async_remote_copy(
            src_ref=to_mem.at[j], dst_ref=recv.at[slot],
            send_sem=mem_s.at[j], recv_sem=mem_r.at[slot],
            device_id=(grp, j), device_id_type=MESH,
        )

    return to_sibling, to_across, to_member


def synth_body(
    groups, members, spec_hbm, inv_hbm, leg_hbm, deg_ref, ord_ref, *refs
):
    outs, refs = refs[: len(CHUNKS)], refs[len(CHUNKS) :]
    spec, inv, leg_ref, t0, t1, t2, main, rest, solved, f0, f1, f2, sems = refs[:13]
    refs = refs[13:]
    buffers = [refs[i * SLOTS : (i + 1) * SLOTS] for i in range(len(CHUNKS))]
    refs = refs[SLOTS * len(CHUNKS) :]
    sem_sets = [refs[i * 6 : (i + 1) * 6] for i in range(len(CHUNKS))]

    orders, radii, width = spec.shape[2:]
    shells = inv.shape[0]
    lats = leg_ref.shape[1]
    half = LANES // 2
    mine = shells // groups
    per_tile = LANES // orders
    pitch, lat_pitch = width + 1, orders + 1

    grp, me = lax.axis_index("grp"), lax.axis_index("mem")
    y, core = grp // 2, grp % 2
    sibling = y * 2 + (1 - core)
    across = (1 - y) * 2 + core
    place = (grp, me, core, sibling, across)

    barrier = pltpu.get_barrier_semaphore()
    for g in (sibling, across):
        pl.semaphore_signal(barrier, inc=1, device_id=(g, me), device_id_type=MESH)
    for i in range(1, members):
        pl.semaphore_signal(
            barrier, inc=1, device_id=(grp, (me + i) % members), device_id_type=MESH
        )

    pieces = 3 if shells % 6 == 0 else 1
    piece = shells // pieces
    inv_copies = [
        pltpu.make_async_copy(
            inv_hbm.at[pl.ds(i * piece, piece)], inv.at[pl.ds(i * piece, piece)], sems.at[4 + i]
        )
        for i in range(pieces)
    ]
    for copy in inv_copies:
        copy.start()
    copies = [pltpu.make_async_copy(spec_hbm.at[c], spec.at[c], sems.at[c]) for c in range(3)]
    leg_copy = pltpu.make_async_copy(leg_hbm, leg_ref, sems.at[3])
    for copy in (*copies, leg_copy):
        copy.start()

    eye = (
        lax.broadcasted_iota(jnp.int32, (2 * width, 2 * width), 0)
        == lax.broadcasted_iota(jnp.int32, (2 * width, 2 * width), 1)
    ).astype(BF16)

    def turn_inverse(i, carry):
        both = jnp.concatenate([inv[2 * i], inv[2 * i + 1]], axis=1)
        out = nt(eye, jnp.concatenate([both, both[LANES:]], axis=0))
        for h in range(2):
            at = pl.ds((2 * i + h) * pitch, width)
            part = out[h * width : (h + 1) * width]
            main[at, :] = part[:, 0:LANES]
            rest[at, :] = part[:, LANES : 2 * LANES]
        return carry

    for i, copy in enumerate(inv_copies):
        copy.wait()
        lax.fori_loop(i * piece // 2, (i + 1) * piece // 2, turn_inverse, 0, unroll=8)

    def turn(c):
        copies[c].wait()

        def turn_profiles(i, carry):
            stack = []
            for p in range(2):
                m = 4 * i + 2 * p
                a, b = [
                    jnp.concatenate([spec[c, k, m], spec[c, k, m + 1]], axis=1)
                    for k in range(2)
                ]
                stack += [a, b[LANES:], b[:LANES]]
            out = nt(eye, jnp.concatenate(stack, axis=0))
            for p in range(2):
                for h in range(2):
                    at = pl.ds((c * orders + 4 * i + 2 * p + h) * pitch, width)
                    part = out[h * width : (h + 1) * width]
                    for n, to in enumerate((t0, t1, t2)):
                        to[at, :] = part[:, (3 * p + n) * LANES : (3 * p + n + 1) * LANES]
            return carry

        lax.fori_loop(0, orders // 4, turn_profiles, 0, unroll=4)

    pad = jnp.zeros((half - shells, 2 * LANES), BF16)

    def solve_chunk(comps):
        count = len(comps) * orders
        low = lax.broadcasted_iota(jnp.int32, (count, LANES), 1) < half

        def solve(l, carry):
            at = pl.ds(comps[0] * orders * pitch + l, count, stride=pitch)
            shared = t1[at, :]
            real = jnp.concatenate([t0[at, :], jnp.where(low, shared, 0.0)], axis=1)
            imag = jnp.concatenate([t2[at, :], jnp.where(low, 0.0, shared)], axis=1)
            profiles = jnp.concatenate([real, imag], axis=0).astype(BF16)
            on = pl.ds(l, shells, stride=pitch)
            weights = jnp.concatenate([main[on, :], rest[on, :]], axis=1).astype(BF16)
            out = nt(profiles, jnp.concatenate([weights, pad], axis=0))
            solved[at, :] = jnp.concatenate([out[:count], out[count:]], axis=1)
            return carry

        lax.fori_loop(0, width, solve, 0, unroll=16)

    degrees = deg_ref[pl.ds(pl.multiple_of(grp * width, width), width)].reshape(1, width)
    sums = (f0, f1, f2)

    def sum_chunk(comps):
        def sum_degrees(m, carry):
            valid = degrees >= ord_ref[me * orders + m]
            table = jnp.where(valid, leg_ref[m].astype(F32), 0.0).astype(BF16)
            block = jnp.concatenate(
                [
                    solved[pl.ds((c * orders + m) * pitch, width), :].astype(BF16)
                    for c in comps
                ],
                axis=1,
            )
            out = nn(table, block)
            at = pl.ds(m, lats, stride=lat_pitch)
            for i, c in enumerate(comps):
                sums[c][at, :] = out[:, i * LANES : (i + 1) * LANES]
            return carry

        lax.fori_loop(0, orders, sum_degrees, 0, unroll=16)

    row = lax.broadcasted_iota(jnp.int32, (2 * shells, LANES), 0)
    lane = lax.broadcasted_iota(jnp.int32, (2 * shells, LANES), 1)
    want = row
    for i in range(1, 2 * groups):
        g, k = i // 2, i % 2
        step = (half + g * mine - i * mine) if k else (g * mine - i * mine)
        want = jnp.where(row >= i * mine, row + step, want)
    pick = (want == lane).astype(BF16)
    tiles = lats // members // per_tile

    def target(i):
        return (me + 1 + i) % members

    def pair_sum(n, j, which):
        send_ref, from_sib = buffers[n][:2]
        return send_ref[j, core, which].astype(F32) + from_sib[j, which].astype(F32)

    def send_chunk(n):
        send_ref, _, to_far = buffers[n][:3]
        to_sibling, to_across, _ = transfers(buffers[n][1:], sem_sets[n], send_ref, place)
        lag = 2

        def first(i):
            j = target(i)
            parts = []
            for b in range(tiles):
                at = [
                    pl.ds(((j * tiles + b) * per_tile + i) * lat_pitch, orders)
                    for i in range(per_tile)
                ]
                for c in CHUNKS[n]:
                    both = jnp.concatenate([sums[c][a, :].astype(BF16) for a in at], axis=0)
                    parts.append(nt(pick, both))
            for g in range(groups):
                block = [p[g * 2 * mine : (g + 1) * 2 * mine] for p in parts]
                send_ref[j, g % 2, g // 2] = jnp.concatenate(block, axis=0).astype(BF16)
            to_sibling(j).start()

        def second(i):
            j = target(i)
            to_sibling(j).wait_recv()
            to_far[j] = pair_sum(n, j, 1 - y).astype(BF16)
            to_across(j).start()

        def step(i, carry):
            first(i + lag)
            second(i)
            return carry

        for i in range(lag):
            first(i)
        lax.fori_loop(0, members - lag, step, 0)
        for i in range(members - lag, members):
            second(i)

    def third(n):
        _, to_across, to_member = transfers(buffers[n][1:], sem_sets[n], buffers[n][0], place)
        _, _, _, from_far, to_mem, _ = buffers[n]

        def total(j):
            to_across(j).wait_recv()
            return (pair_sum(n, j, y) + from_far[j].astype(F32)).astype(BF16)

        def step(i, carry):
            j = target(i)
            to_mem[j] = total(j)
            to_member(j, me).start()
            return carry

        lax.fori_loop(0, members - 1, step, 0)
        outs[n][me] = total(me)

    def finish(n):
        moves = transfers(buffers[n][1:], sem_sets[n], buffers[n][0], place)
        to_sibling, to_across, to_member = moves
        recv = buffers[n][5]

        def step(i, carry):
            j = target(i)
            to_member(j, j).wait_recv()
            outs[n][j] = recv[j]
            to_member(j, me).wait_send()
            return carry

        lax.fori_loop(0, members - 1, step, 0)

        def drain(i, carry):
            to_sibling(i).wait_send()
            to_across(i).wait_send()
            return carry

        lax.fori_loop(0, members, drain, 0)

    last = len(CHUNKS) - 1
    for n, comps in enumerate(CHUNKS):
        for c in comps:
            turn(c)
        solve_chunk(comps)
        if n:
            third(n - 1)
        if n == 0:
            leg_copy.wait()
        sum_chunk(comps)
        if n == 0:
            pl.semaphore_wait(barrier, members + 1)
        send_chunk(n)
    third(last)
    for n in range(len(CHUNKS)):
        finish(n)


def synthesize(spec, inv, legendre, degree_list, order_map, groups, members):
    _, _, orders, radii, width = spec.shape
    shells = inv.shape[0]
    lats = legendre.shape[1]
    mine = shells // groups
    pitch = width + 1
    any_space = pl.BlockSpec(memory_space=pl.ANY)
    vmem = pl.BlockSpec(memory_space=pltpu.VMEM)
    buffers, shapes = [], []
    for comps in CHUNKS:
        block = lats // members * orders * mine * 2 * len(comps) // LANES
        slots = pltpu.VMEM((members, block, LANES), BF16)
        buffers += [
            pltpu.VMEM((members, 2, groups // 2, block, LANES), BF16),
            pltpu.VMEM((members, groups // 2, block, LANES), BF16),
            slots, slots, slots, slots,
        ]
        shapes.append(jax.ShapeDtypeStruct((members, block, LANES), BF16))
    return pl.pallas_call(
        functools.partial(synth_body, groups, members),
        out_shape=shapes,
        in_specs=[any_space] * 3 + [vmem, pl.BlockSpec(memory_space=pltpu.SMEM)],
        out_specs=[vmem] * len(CHUNKS),
        scratch_shapes=[
            pltpu.VMEM(spec.shape, BF16),
            pltpu.VMEM(inv.shape, BF16),
            pltpu.VMEM(legendre.shape, BF16),
            *[pltpu.VMEM((3 * orders * pitch, LANES), F32)] * 3,
            *[pltpu.VMEM((shells * pitch, LANES), F32)] * 2,
            pltpu.VMEM((3 * orders * pitch, LANES), F32),
            *[pltpu.VMEM((lats * (orders + 1), LANES), F32)] * 3,
            pltpu.SemaphoreType.DMA((7,)),
            *buffers,
            *[pltpu.SemaphoreType.DMA((members,))] * (6 * len(CHUNKS)),
        ],
        compiler_params=pltpu.CompilerParams(
            collective_id=0, has_side_effects=True, vmem_limit_bytes=60 * 2**20
        ),
        name="synthesize",
    )(spec, inv, legendre, degree_list, order_map)


def cos_sin(phase, count):
    phase = phase - count * jnp.floor((phase + 0.5) * (1.0 / count))
    turns = jnp.floor((phase + count / 8) * (4.0 / count))
    t = (phase - turns * (count / 4)) * (2.0 * math.pi / count)
    x = t * t
    s = t * (1 + x * (-1 / 6 + x * (1 / 120 + x * (-1 / 5040 + x * (1 / 362880)))))
    c = 1 + x * (
        -1 / 2 + x * (1 / 24 + x * (-1 / 720 + x * (1 / 40320 + x * (-1 / 3628800))))
    )
    odd = (turns == 1) | (turns == 3)
    cos, sin = jnp.where(odd, s, c), jnp.where(odd, c, s)
    cos = jnp.where((turns == 1) | (turns == 2), -cos, cos)
    sin = jnp.where((turns == 2) | (turns == 3), -sin, sin)
    return cos, sin


def physical_body(orders, wide, *refs):
    recvs, refs = refs[: len(CHUNKS)], refs[len(CHUNKS) :]
    vort_hbm, ord_ref, out_hbm, vort_ref, made, sem, *keep = refs
    held, keep = keep[: len(CHUNKS)], keep[len(CHUNKS) :]
    copy = pltpu.make_async_copy(vort_hbm, vort_ref, sem.at[0])
    arrivals = [
        pltpu.make_async_copy(r, h, sem.at[1 + n]) for n, (r, h) in enumerate(zip(recvs, held))
    ]
    for arrival in arrivals:
        arrival.start()
    copy.start()
    members = recvs[0].shape[0]
    shells = vort_ref.shape[1]
    lats = vort_ref.shape[2]
    points = vort_ref.shape[3]
    every = members * orders
    per_tile = LANES // orders
    tiles = lats // per_tile
    line = ord_ref[...].reshape(1, every).astype(F32)
    same = lax.broadcasted_iota(jnp.int32, (every, every), 0) == lax.broadcasted_iota(
        jnp.int32, (every, every), 1
    )
    column = jnp.sum(jnp.where(same, line, 0.0), axis=1, keepdims=True)
    lane = lax.broadcasted_iota(jnp.int32, (every, LANES), 1).astype(F32)
    nc, ns = cos_sin(column * lane, points)
    weight = jnp.where(column == 0.0, 1.0, 2.0)
    nc, ns = weight * nc, weight * ns
    far_c, far_s = cos_sin(column * (lane * LANES), points)

    for arrival in arrivals:
        arrival.wait()
    for comps, recv_ref in zip(CHUNKS, held):
        for i in range(per_tile):
            for h in range(members // per_tile):
                parts = [
                    recv_ref[h * per_tile + j].astype(F32)[:, i * orders : (i + 1) * orders]
                    for j in range(per_tile)
                ]
                joined = jnp.concatenate(parts, axis=1)
                for b in range(tiles):
                    for n, c in enumerate(comps):
                        for k in range(2):
                            at = ((b * len(comps) + n) * 2 + k) * shells
                            to = pl.ds(
                                c * shells * lats + b * per_tile + i, shells, stride=lats
                            )
                            keep[k * (members // per_tile) + h][to, :] = joined[at : at + shells]
    left = jnp.concatenate([r[...].astype(BF16) for r in keep], axis=1)

    flat = shells * lats
    shape = (shells, lats, wide)
    copy.wait()
    writes = []
    for q in range(points // wide):
        on = pl.ds(q * wide, wide)
        tables = []
        for p in range(q * wide // LANES, (q + 1) * wide // LANES):
            fc, fs = far_c[:, p : p + 1], far_s[:, p : p + 1]
            tables.append(jnp.concatenate([nc * fc - ns * fs, -(ns * fc + nc * fs)], axis=0))
        v = nn(left, jnp.concatenate(tables, axis=1).astype(BF16))
        v0, v1, v2 = v[:flat], v[flat : 2 * flat], v[2 * flat :]
        w0, w1, w2 = [vort_ref[c, :, :, on].reshape(flat, wide).astype(F32) for c in range(3)]
        made[0, :, :, on] = (v1 * w2 - v2 * w1).astype(BF16).reshape(shape)
        made[1, :, :, on] = (v2 * w0 - v0 * w2).astype(BF16).reshape(shape)
        made[2, :, :, on] = (v0 * w1 - v1 * w0).astype(BF16).reshape(shape)
        writes.append(
            pltpu.make_async_copy(
                made.at[:, :, :, on], out_hbm.at[:, :, :, on], sem.at[1 + len(CHUNKS) + q]
            )
        )
        writes[-1].start()
    for write in writes:
        write.wait()


def physical(received, vorticity, order_map, orders):
    members = received[0].shape[0]
    _, shells, lats, points = vorticity.shape
    wide = 2 * LANES if points % (2 * LANES) == 0 else LANES
    vmem = pl.BlockSpec(memory_space=pltpu.VMEM)
    return pl.pallas_call(
        functools.partial(physical_body, orders, wide),
        out_shape=jax.ShapeDtypeStruct(vorticity.shape, BF16),
        in_specs=[pl.BlockSpec(memory_space=pl.ANY)] * (len(CHUNKS) + 1) + [vmem],
        out_specs=pl.BlockSpec(memory_space=pl.ANY),
        scratch_shapes=[
            pltpu.VMEM(vorticity.shape, BF16),
            pltpu.VMEM(vorticity.shape, BF16),
            pltpu.SemaphoreType.DMA((1 + len(CHUNKS) + points // wide,)),
        ]
        + [pltpu.VMEM(r.shape, BF16) for r in received]
        + [pltpu.VMEM((3 * shells * lats, LANES), F32)] * (2 * members * orders // LANES),
        compiler_params=pltpu.CompilerParams(vmem_limit_bytes=60 * 2**20),
        name="physical",
    )(*received, vorticity, order_map)


def shards(groups, members, spectral, inverse, legendre, vorticity, degree_list, order_map):
    orders = spectral.shape[3]
    spec = jnp.transpose(spectral, (1, 2, 3, 4, 0))
    inv = jnp.transpose(inverse, (1, 2, 0))
    vort = jnp.transpose(vorticity, (0, 2, 1, 3))
    received = synthesize(spec, inv, legendre, degree_list, order_map, groups, members)
    out = physical(received, vort, order_map, orders)
    return jnp.transpose(out, (0, 2, 1, 3))


def solution(mesh):
    groups, members = mesh.shape["grp"], mesh.shape["mem"]

    def local(spectral, inverse, legendre, vorticity, degree_list, order_map):
        args = (spectral, inverse, legendre, vorticity, degree_list, order_map)
        width, _, _, orders, radii = spectral.shape
        shells, lats = inverse.shape[1], legendre.shape[1]
        fits = (
            groups == 4
            and width == LANES
            and 2 * shells <= LANES
            and LANES < radii
            and 2 * radii == 3 * LANES
            and LANES % orders == 0
            and orders % 4 == 0
            and shells % 2 == 0
            and (shells // groups * 2) % 8 == 0
            and members % (LANES // orders) == 0
            and (lats // members) % (LANES // orders) == 0
            and vorticity.shape[3] % LANES == 0
            and vorticity.shape[3] // LANES <= LANES
            and members * orders * vorticity.shape[3] < 2**23
            and (lats // members) * orders * (shells // groups) * 2 % (16 * LANES) == 0
        )
        if fits:
            return shards(groups, members, *args)
        return plain_shards(*args)

    return jax.shard_map(
        local,
        mesh=mesh,
        in_specs=(
            P("grp", None, None, "mem", None),
            P("grp", None, None),
            P("mem", None, "grp"),
            P(None, "mem", "grp", None),
            P(),
            P(),
        ),
        out_specs=P(None, "mem", "grp", None),
        check_vma=False,
    )
```
